32 devices in a mesh: groups: 2 (over x), seq: 16 (over z, y, core).
Axes of the slice: x: 2, y: 2, z: 4, core: 2. Of those that a mesh axis runs over, the one named last changes fastest.
Arguments:
- queries: bfloat16 [8192, 1280], P(('groups', 'seq')), parts along dimension 0, may hold values from -6 to 6
- keys: bfloat16 [8192, 1280], P(('groups', 'seq')), parts along dimension 0, may hold values from -6 to 6
- values: bfloat16 [8192, 1280], P(('groups', 'seq')), parts along dimension 0, may hold values from -6 to 6
- cotangent: bfloat16 [8192, 1280], P(('groups', 'seq')), parts along dimension 0, may hold values from -6 to 6
- local_blocks: int32 [64, 3], P('groups'), parts along dimension 0, may hold values from -1 to 31, as said below
- far_blocks: int32 [64, 4], P('groups'), parts along dimension 0, may hold values from -1 to 29, as said below
- counts: int32 [64], P('groups'), parts along dimension 0, may hold values from 2 to 128
Outputs:
- attended: bfloat16 [8192, 1280], P(('groups', 'seq')), parts along dimension 0
- grad_queries: bfloat16 [8192, 1280], P(('groups', 'seq')), parts along dimension 0
- grad_keys: bfloat16 [8192, 1280], P(('groups', 'seq')), parts along dimension 0
- grad_values: bfloat16 [8192, 1280], P(('groups', 'seq')), parts along dimension 0
The draws below stay inside these ranges and needn't reach their ends.
There are 2 independent parts, one for each index of `groups`. The reference program is written for one: setup_inputs(seed, part) draws one part's arguments, and reference() takes and returns one part's arrays. A program takes and returns all parts, laid end to end along the dimension named above; each array names one. Nothing has to cross between parts.
Inputs may be any that keep to these rules, and one draw needn't show every extreme that they name: `local_blocks`: row b holds block b itself first, then 3 - 1 distinct blocks whose index differs from b by 1 to 2, or -1 where such a block lies outside the sequence. `far_blocks`: each entry of row b is -1 or a block whose index lies in [(b // 2 - k) * 2, (b // 2 - k + 1) * 2) for some k from 1 to 2; it is -1 exactly where that range would start below 0. Entries may repeat.
All inputs are finite; a program needn't handle non-finite values.
Results may differ from the reference program's by a relative error of at most 0.027.
Values may be sent and summed in bfloat16 or wider, within the bound.
No kernel may reach another device: no remote copies, remote signals or barrier semaphores. Data moves between devices by JAX's collectives and lax.ppermute only.
A program may use at most 128 MiB of HBM per device.

```python
import math
import jax
import jax.numpy as jnp
from jax import lax

D = 1280
HEADS = 16
BLK = 128
LR = 2
NLOC = 3
NFAR = 4
HOPS = 2
TOKENS = 4096
NBLK = 32
NB_DEV = 2


def background(key, marker):
    return jnp.clip(jax.random.normal(jax.random.fold_in(key, marker), (TOKENS, D)), -6.0, 6.0)


def draw_queries(key, part):
    drawn = background(key, 1).reshape(NBLK, BLK, D)
    return drawn.reshape(TOKENS, D).astype(jnp.bfloat16)


def draw_keys(key, part):
    drawn = background(key, 5).reshape(NBLK, BLK, D)
    return drawn.reshape(TOKENS, D).astype(jnp.bfloat16)


def draw_local_blocks(key, part):
    others = jnp.concatenate((jnp.arange(-LR, 0, dtype=jnp.int32), jnp.arange(1, LR + 1, dtype=jnp.int32)))
    ranking = jax.random.randint(jax.random.fold_in(key, 11), (NBLK, 2 * LR), 0, 1 << 20)
    ordering = jnp.argsort(ranking, axis=1, stable=True)
    picked = others[ordering[:, :NLOC - 1]]
    offsets = jnp.concatenate((jnp.zeros((NBLK, 1), jnp.int32), picked), axis=1)
    target = jnp.arange(NBLK, dtype=jnp.int32)[:, None] + offsets
    return jnp.where((target >= 0) & (target < NBLK), target, -1).astype(jnp.int32)


def draw_far_blocks(key, part):
    hop_count = jax.random.randint(jax.random.fold_in(key, 21), (NBLK, NFAR), 1, HOPS + 1)
    within = jax.random.randint(jax.random.fold_in(key, 22), (NBLK, NFAR), 0, NB_DEV)
    source = jnp.arange(NBLK, dtype=jnp.int32)[:, None] // NB_DEV - hop_count
    return jnp.where(source >= 0, source * NB_DEV + within, -1).astype(jnp.int32)


def place_ends(values, rng, smallest, high):
    spot = [jax.random.randint(jax.random.fold_in(rng, axis), (), 0, length) for axis, length in enumerate(values.shape)]
    main_axis = values.shape.index(max(values.shape))
    beside = spot[:main_axis] + [(spot[main_axis] + 1) % values.shape[main_axis]] + spot[main_axis + 1:]
    return values.at[tuple(spot)].set(smallest).at[tuple(beside)].set(high)


def levels(stream_key, shape, pieces, least, largest):
    loudness = 1.0
    for dim, shards_of in pieces:
        heights = jax.random.uniform(jax.random.fold_in(jax.random.fold_in(stream_key, 6), dim), (shards_of,), jnp.float32, least / len(pieces), largest / len(pieces))
        loudness = loudness * jnp.repeat(jnp.exp(heights), shape[dim] // shards_of).reshape((-1,) + (1,) * (len(shape) - 1 - dim))
    return loudness


def noise(rng, shape, scale, reach, shards=(), held_as=jnp.bfloat16):
    values = jax.random.normal(rng, shape, jnp.float32) * scale
    if len(shards) > 0:
        values = levels(rng, shape, shards, -0.22, 0.18) * values
    return jnp.clip(values, min=-reach, max=reach).astype(held_as)


def setup_inputs(seed: int = 0, part: int = 0) -> dict:
    splits = jax.random.split(jax.random.key(seed), 8)
    part_keys = jax.random.split(jax.random.fold_in(splits[7], part), 8)
    return {
        "queries": draw_queries(jax.random.fold_in(jax.random.fold_in(splits[7], part), 71), part),
        "keys": draw_keys(jax.random.fold_in(jax.random.fold_in(splits[7], part), 71), part),
        "values": noise(part_keys[2], (TOKENS, D), 1.0, 6.0, ((0, 16),)),
        "cotangent": noise(part_keys[3], (TOKENS, D), 1.0, 6.0, ((0, 16),)),
        "local_blocks": draw_local_blocks(jax.random.fold_in(jax.random.fold_in(splits[7], part), 71), part),
        "far_blocks": draw_far_blocks(jax.random.fold_in(jax.random.fold_in(splits[7], part), 71), part),
        "counts": place_ends(jax.random.randint(part_keys[6], (NBLK,), 2, BLK + 1), jax.random.fold_in(part_keys[6], 1), 2, BLK).astype(jnp.int32),
    }


def reference(queries, keys, values, cotangent, local_blocks, far_blocks, counts):
    total_rows, model_width = queries.shape
    head_size = model_width // HEADS
    block_total = total_rows // BLK
    slot_total = NLOC + NFAR
    score_scale = 1.0 / math.sqrt(head_size)
    highest = lax.Precision.HIGHEST
    listing = jnp.concatenate((local_blocks, far_blocks), axis=1).astype(jnp.int32)
    position = jnp.arange(BLK, dtype=jnp.int32)
    slot_order = jnp.arange(slot_total, dtype=jnp.int32)

    def one_block(carried, block_id):
        key_sums, value_sums = carried
        chosen = lax.dynamic_index_in_dim(listing, block_id, 0, keepdims=False)
        repeated = jnp.any((chosen[:, None] == chosen[None, :]) & (slot_order[None, :] < slot_order[:, None]), axis=1)
        slot_live = (chosen >= 0) & jnp.logical_not(repeated)
        safe_index = jnp.maximum(chosen, 0).astype(jnp.int32)
        key_count = counts[safe_index]
        key_mask = (slot_live[:, None] & (position[None, :] < key_count[:, None])).reshape(-1)
        key_rows = (safe_index[:, None] * BLK + position[None, :]).reshape(-1).astype(jnp.int32)
        near_keys = keys[key_rows].astype(jnp.float32).reshape(-1, HEADS, head_size)
        near_values = values[key_rows].astype(jnp.float32).reshape(-1, HEADS, head_size)
        first_row = (block_id * BLK).astype(jnp.int32)
        block_query = lax.dynamic_slice_in_dim(queries, first_row, BLK, 0).astype(jnp.float32).reshape(BLK, HEADS, head_size)
        block_grad = lax.dynamic_slice_in_dim(cotangent, first_row, BLK, 0).astype(jnp.float32)
        grad_heads = block_grad.reshape(BLK, HEADS, head_size)
        scores = jnp.einsum('qhd,khd->hqk', block_query, near_keys, precision=highest) * score_scale
        masked = jnp.where(key_mask[None, None, :], scores, -jnp.inf)
        row_peak = lax.optimization_barrier(jnp.max(masked, axis=2, keepdims=True))
        row_total = lax.optimization_barrier(jnp.sum(jnp.where(key_mask[None, None, :], jnp.exp(scores - row_peak), 0.0), axis=2, keepdims=True))
        log_total = row_peak + jnp.log(row_total)
        chance = jnp.where(key_mask[None, None, :], jnp.exp(scores - log_total), 0.0)
        weights = lax.optimization_barrier(chance.astype(jnp.bfloat16)).astype(jnp.float32)
        block_out = jnp.einsum('hqk,khd->qhd', weights, near_values, precision=highest).reshape(BLK, model_width).astype(jnp.bfloat16)
        out_wide = lax.optimization_barrier(block_out).astype(jnp.float32)
        row_delta = lax.optimization_barrier(jnp.sum((block_grad * out_wide).reshape(BLK, HEADS, head_size), axis=2)).T
        grad_chance = jnp.einsum('qhd,khd->hqk', grad_heads, near_values, precision=highest)
        grad_scores = chance * (grad_chance - row_delta[:, :, None])
        grad_scores = lax.optimization_barrier(grad_scores.astype(jnp.bfloat16)).astype(jnp.float32)
        query_part = (jnp.einsum('hqk,khd->qhd', grad_scores, near_keys, precision=highest) * score_scale).reshape(BLK, model_width).astype(jnp.bfloat16)
        key_part = (jnp.einsum('hqk,qhd->khd', grad_scores, block_query, precision=highest) * score_scale).reshape(-1, model_width)
        value_part = jnp.einsum('hqk,qhd->khd', weights, grad_heads, precision=highest).reshape(-1, model_width)
        key_sums = key_sums.at[key_rows].add(key_part)
        value_sums = value_sums.at[key_rows].add(value_part)
        return ((key_sums, value_sums), (block_out, query_part))
    empty = jnp.zeros((total_rows, model_width), jnp.float32)
    sums, outputs = lax.scan(one_block, (empty, empty), jnp.arange(block_total, dtype=jnp.int32))
    attended = outputs[0].reshape(total_rows, model_width)
    grad_queries = outputs[1].reshape(total_rows, model_width)
    return (attended, grad_queries, sums[0].astype(jnp.bfloat16), sums[1].astype(jnp.bfloat16))
```

```python
import math

import jax
import jax.numpy as jnp
from jax import lax
from jax.experimental import pallas as pl
from jax.experimental.pallas import tpu as pltpu
from jax.sharding import PartitionSpec as P

HEADS = 16
BLK = 128
PLANE = 4
CHUNKS = (2, 2)
FAR_UP = 2
WINDOW = 4
CHAIN = PLANE + FAR_UP + 1
F32 = jnp.float32
BF16 = jnp.bfloat16
ANY = pl.BlockSpec(memory_space=pl.ANY)
SMEM = pl.BlockSpec(memory_space=pltpu.SMEM)
VMEM = pl.BlockSpec(memory_space=pltpu.VMEM)


def params(mib=48):
    return pltpu.CompilerParams(vmem_limit_bytes=mib << 20)


def run_copies(copies):
    for copy in copies:
        copy.start()
    for copy in copies:
        copy.wait()


def prep_kernel(head_size, roles, *refs):
    inputs = refs[:4]
    outs = refs[4 : 4 + PLANE * len(CHUNKS)]
    turned, sems = refs[4 + PLANE * len(CHUNKS) :]
    for index, ref in enumerate(inputs):
        turned[index] = ref[...].T
    place = roles[0]
    copies = []
    per_device = HEADS // PLANE
    first = 0
    for chunk, heads in enumerate(CHUNKS):
        for hop in range(PLANE):
            group = place ^ hop
            row = pl.multiple_of((group * per_device + first) * head_size, 16)
            number = chunk * PLANE + hop
            copies.append(
                pltpu.make_async_copy(
                    turned.at[:, pl.ds(row, heads * head_size)], outs[number], sems.at[number]
                )
            )
        first += heads
    run_copies(copies)


def limits_kernel(roles, local_blocks, far_blocks, counts, out):
    blocks = counts.shape[0]
    first = roles[1] * (PLANE * 2)
    for query in range(PLANE * 2):
        listed = [local_blocks[first + query, s] for s in range(local_blocks.shape[1])]
        listed += [far_blocks[first + query, s] for s in range(far_blocks.shape[1])]
        for slot in range(WINDOW * 2):
            key = first - 2 * FAR_UP + (query // 2) * 2 + slot
            found = listed[0] == key
            for entry in listed[1:]:
                found = found | (entry == key)
            inside = (key >= 0) & (key < blocks)
            count = counts[jnp.clip(key, 0, blocks - 1)]
            out[query * WINDOW * 2 + slot] = jnp.where(found & inside, count, 0)


def pack_kernel(roles, *refs):
    pieces = refs[:PLANE]
    even, odd = refs[PLANE : PLANE + 2]
    plane, sems = refs[PLANE + 2 :]
    place, parity = roles[0], roles[2]
    run_copies(
        [
            pltpu.make_async_copy(
                pieces[hop].at[pl.ds(0, 2)], plane.at[place ^ hop], sems.at[hop]
            )
            for hop in range(PLANE)
        ]
    )
    run_copies(
        [
            pltpu.make_async_copy(plane.at[pl.ds(2 - 2 * parity, 2)], even, sems.at[0]),
            pltpu.make_async_copy(plane.at[pl.ds(2 * parity, 2)], odd, sems.at[1]),
        ]
    )


def dot(a, b, left, right):
    return lax.dot_general(a, b, (((left,), (right,)), ((), ())), preferred_element_type=F32)


def main_kernel(head_size, heads, roles, limits, *refs):
    pieces = refs[:PLANE]
    even_in, odd_in = refs[PLANE : PLANE + 2]
    rest = refs[PLANE + 2 :]
    outs = rest[:PLANE]
    local_out, even_out, odd_out = rest[PLANE : PLANE + 3]
    chain, query, result, key_sums, sums, sems = rest[PLANE + 3 :]
    place, parity = roles[0], roles[2]
    copies = []
    for hop in range(PLANE):
        unit = place ^ hop
        copies.append(
            pltpu.make_async_copy(
                pieces[hop].at[pl.ds(0, 2)], chain.at[FAR_UP + unit], sems.at[2 * hop]
            )
        )
        copies.append(
            pltpu.make_async_copy(
                pieces[hop].at[pl.ds(2, 2)], query.at[unit], sems.at[2 * hop + 1]
            )
        )
    above = FAR_UP + PLANE
    copies.append(
        pltpu.make_async_copy(
            even_in, chain.at[pl.ds((1 - parity) * above, 2)], sems.at[2 * PLANE]
        )
    )
    copies.append(
        pltpu.make_async_copy(odd_in, chain.at[pl.ds(parity * above, 2)], sems.at[2 * PLANE + 1])
    )
    for copy in copies:
        copy.start()
    key_sums[...] = jnp.zeros_like(key_sums)
    for copy in copies:
        copy.wait()

    scale = 1.0 / math.sqrt(head_size)
    rate = scale * math.log2(math.e)
    tokens = 2 * BLK
    row = lax.broadcasted_iota(jnp.int32, (BLK, tokens), 0)
    lane = lax.broadcasted_iota(jnp.int32, (1, tokens), 1)

    def step(index, carry):
        head, unit = index // PLANE, index % PLANE
        query_t = query[unit, 0, head]
        grad_t = query[unit, 1, head]
        scores = []
        peak = jnp.full((1, tokens), -1e30, F32)
        for k in range(WINDOW):
            tile = dot(chain[unit + k, 0, head], query_t, 0, 0)
            for half in range(2):
                slot = 2 * k + half
                base = unit * 2 * WINDOW * 2 + slot
                limit = jnp.where(lane < BLK, limits[base], limits[base + WINDOW * 2])
                part = jnp.where(row < limit, tile[half * BLK : (half + 1) * BLK], -1e30)
                peak = jnp.maximum(peak, jnp.max(part, axis=0, keepdims=True))
                scores.append(part)
        total = jnp.zeros((1, tokens), F32)
        powers = []
        for part in scores:
            power = jnp.exp2((part - peak) * rate)
            total = total + jnp.sum(power, axis=0, keepdims=True)
            powers.append(power)
        powers = [
            jnp.concatenate(powers[2 * k : 2 * k + 2], axis=0) for k in range(WINDOW)
        ]
        weights = [power.astype(BF16) for power in powers]
        inverse = 1.0 / total
        out_t = dot(chain[unit, 1, head], weights[0], 1, 0)
        for k in range(1, WINDOW):
            out_t = out_t + dot(chain[unit + k, 1, head], weights[k], 1, 0)
        attended = (out_t * inverse).astype(BF16)
        grad_wide = grad_t.astype(F32)
        delta = jnp.sum(grad_wide * attended.astype(F32), axis=0, keepdims=True) * inverse
        grad_scaled = (grad_wide * inverse).astype(BF16)
        query_grad = jnp.zeros((head_size, tokens), F32)
        for k in range(WINDOW):
            grad_chance = dot(chain[unit + k, 1, head], grad_scaled, 0, 0)
            grad_scores = (powers[k] * (grad_chance - delta)).astype(BF16)
            query_grad = query_grad + dot(chain[unit + k, 0, head], grad_scores, 1, 0)
            key_sums[unit + k, 0, head] += dot(query_t, grad_scores, 1, 1)
            key_sums[unit + k, 1, head] += dot(grad_scaled, weights[k], 1, 1)
        result[unit, 0, head] = attended
        result[unit, 1, head] = (query_grad * scale).astype(BF16)
        return carry

    lax.fori_loop(0, heads * PLANE, step, 0)
    for unit in range(CHAIN + 1):
        sums[unit, 0] = (key_sums[unit, 0] * scale).astype(BF16)
        sums[unit, 1] = key_sums[unit, 1].astype(BF16)
    copies = [
        pltpu.make_async_copy(result.at[place ^ hop], outs[hop], sems.at[hop])
        for hop in range(PLANE)
    ]
    copies.append(
        pltpu.make_async_copy(sums.at[pl.ds(FAR_UP, PLANE)], local_out, sems.at[PLANE])
    )
    copies.append(
        pltpu.make_async_copy(
            sums.at[pl.ds((1 - parity) * above, 2)], even_out, sems.at[PLANE + 1]
        )
    )
    copies.append(
        pltpu.make_async_copy(sums.at[pl.ds(parity * above, 2)], odd_out, sems.at[PLANE + 2])
    )
    run_copies(copies)


def join_kernel(roles, local, even_in, odd_in, *refs):
    outs = refs[:PLANE]
    held, sems = refs[PLANE:]
    place, parity = roles[0], roles[2]
    below_ok, above_ok = roles[3], roles[4]
    held[...] = local[...]

    def take(below, above):
        @pl.when(below_ok == 1)
        def _():
            held[0] = (held[0].astype(F32) + below[0].astype(F32)).astype(BF16)

        @pl.when(above_ok == 1)
        def _():
            for unit in range(2):
                held[2 + unit] = (held[2 + unit].astype(F32) + above[unit].astype(F32)).astype(
                    BF16
                )

    @pl.when(parity == 0)
    def _():
        take(odd_in, even_in)

    @pl.when(parity == 1)
    def _():
        take(even_in, odd_in)

    run_copies(
        [
            pltpu.make_async_copy(held.at[place ^ hop], outs[hop], sems.at[hop])
            for hop in range(PLANE)
        ]
    )


def finish_kernel(head_size, roles, *refs):
    count = PLANE * len(CHUNKS)
    pieces = refs[:count]
    first_out, second_out, turned, sems = refs[count:]
    place = roles[0]
    per_device = HEADS // PLANE
    copies = []
    first = 0
    for chunk, heads in enumerate(CHUNKS):
        for hop in range(PLANE):
            group = place ^ hop
            row = pl.multiple_of((group * per_device + first) * head_size, 16)
            number = chunk * PLANE + hop
            copies.append(
                pltpu.make_async_copy(
                    pieces[number], turned.at[:, pl.ds(row, heads * head_size)], sems.at[number]
                )
            )
        first += heads
    run_copies(copies)
    first_out[...] = turned[0].T
    second_out[...] = turned[1].T


def body(queries, keys, values, cotangent, local_blocks, far_blocks, counts):
    tokens, width = queries.shape
    head_size = width // HEADS
    size = lax.axis_size("seq")
    planes = size // PLANE
    device = lax.axis_index("seq")
    level = device // PLANE
    roles = jnp.stack(
        [
            device % PLANE,
            level,
            level % 2,
            (level > 0).astype(jnp.int32),
            (level < planes - 1).astype(jnp.int32),
        ]
    ).astype(jnp.int32)

    def swap(array, hop):
        pairs = [(i, (i // PLANE) * PLANE + ((i % PLANE) ^ hop)) for i in range(size)]
        return lax.ppermute(array, "seq", pairs)

    def level_swap(array, odd):
        pairs = []
        for i in range(size):
            z = i // PLANE
            other = z + 1 if z % 2 == odd else z - 1
            pairs.append((i, i + (other - z) * PLANE if 0 <= other < planes else i))
        return lax.ppermute(array, "seq", pairs)

    def piece(tensors, heads):
        return jax.ShapeDtypeStruct((tensors, heads * head_size, tokens), BF16)

    pieces = pl.pallas_call(
        lambda *refs: prep_kernel(head_size, *refs),
        out_shape=[piece(4, heads) for heads in CHUNKS for _ in range(PLANE)],
        in_specs=[SMEM] + [VMEM] * 4,
        out_specs=[ANY] * (PLANE * len(CHUNKS)),
        scratch_shapes=[
            pltpu.VMEM((4, width, tokens), BF16),
            pltpu.SemaphoreType.DMA((PLANE * len(CHUNKS),)),
        ],
        compiler_params=params(),
    )(roles, keys, values, queries, cotangent)
    limits = pl.pallas_call(
        limits_kernel,
        out_shape=jax.ShapeDtypeStruct((PLANE * 2 * WINDOW * 2,), jnp.int32),
        in_specs=[SMEM] * 4,
        out_specs=SMEM,
    )(roles, local_blocks, far_blocks, counts)

    query_pieces = []
    key_pieces = []
    for chunk, heads in enumerate(CHUNKS):
        own = pieces[chunk * PLANE]
        held = [own] + [swap(pieces[chunk * PLANE + hop], hop) for hop in range(1, PLANE)]
        pair = jax.ShapeDtypeStruct((2, 2, heads * head_size, tokens), BF16)
        even, odd = pl.pallas_call(
            pack_kernel,
            out_shape=[pair, pair],
            in_specs=[SMEM] + [ANY] * PLANE,
            out_specs=[ANY, ANY],
            scratch_shapes=[
                pltpu.VMEM((PLANE, 2, heads * head_size, tokens), BF16),
                pltpu.SemaphoreType.DMA((PLANE,)),
            ],
            compiler_params=params(),
        )(roles, *held)
        even, odd = level_swap(even, 0), level_swap(odd, 1)
        shape = (heads, head_size, tokens)
        results = pl.pallas_call(
            lambda *refs, heads=heads: main_kernel(head_size, heads, *refs),
            out_shape=[jax.ShapeDtypeStruct((2,) + shape, BF16)] * PLANE
            + [jax.ShapeDtypeStruct((PLANE, 2) + shape, BF16)]
            + [jax.ShapeDtypeStruct((2, 2) + shape, BF16)] * 2,
            in_specs=[SMEM, SMEM] + [ANY] * (PLANE + 2),
            out_specs=[ANY] * (PLANE + 3),
            scratch_shapes=[
                pltpu.VMEM((CHAIN + 1, 2) + shape, BF16),
                pltpu.VMEM((PLANE, 2) + shape, BF16),
                pltpu.VMEM((PLANE, 2) + shape, BF16),
                pltpu.VMEM((CHAIN + 1, 2) + shape, F32),
                pltpu.VMEM((CHAIN + 1, 2) + shape, BF16),
                pltpu.SemaphoreType.DMA((2 * PLANE + 2,)),
            ],
            compiler_params=params(),
        )(
            roles,
            limits,
            *[part.reshape((4,) + shape) for part in held],
            even.reshape((2, 2) + shape),
            odd.reshape((2, 2) + shape),
        )
        flat = (2, heads * head_size, tokens)
        out = [part.reshape(flat) for part in results[:PLANE]]
        query_pieces += [out[0]] + [swap(out[hop], hop) for hop in range(1, PLANE)]
        local, even, odd = results[PLANE:]
        even, odd = level_swap(even, 0), level_swap(odd, 1)
        back = pl.pallas_call(
            join_kernel,
            out_shape=[piece(2, heads)] * PLANE,
            in_specs=[SMEM] + [VMEM] * 3,
            out_specs=[ANY] * PLANE,
            scratch_shapes=[
                pltpu.VMEM((PLANE,) + flat, BF16),
                pltpu.SemaphoreType.DMA((PLANE,)),
            ],
            compiler_params=params(),
        )(roles, local.reshape((PLANE,) + flat), even.reshape((2,) + flat), odd.reshape((2,) + flat))
        key_pieces += [back[0]] + [swap(back[hop], hop) for hop in range(1, PLANE)]

    def finish(parts):
        return pl.pallas_call(
            lambda *refs: finish_kernel(head_size, *refs),
            out_shape=[jax.ShapeDtypeStruct((tokens, width), BF16)] * 2,
            in_specs=[SMEM] + [ANY] * len(parts),
            out_specs=[VMEM, VMEM],
            scratch_shapes=[
                pltpu.VMEM((2, width, tokens), BF16),
                pltpu.SemaphoreType.DMA((len(parts),)),
            ],
            compiler_params=params(),
        )(roles, *parts)

    attended, query_grad = finish(query_pieces)
    key_grad, value_grad = finish(key_pieces)
    return attended, query_grad, key_grad, value_grad


def solution(mesh):
    rows = P(("groups", "seq"), None)
    return jax.shard_map(
        body,
        mesh=mesh,
        in_specs=(rows, rows, rows, rows, P("groups", None), P("groups", None), P("groups")),
        out_specs=(rows, rows, rows, rows),
        check_vma=False,
    )
```

```python
import math

import jax
import jax.numpy as jnp
from jax import lax
from jax.experimental import pallas as pl
from jax.experimental.pallas import tpu as pltpu
from jax.sharding import PartitionSpec as P

HEADS = 16
BLK = 128
PLANE = 4
CHUNKS = (2, 2)
FAR_UP = 2
WINDOW = 4
CHAIN = PLANE + FAR_UP + 1
F32 = jnp.float32
BF16 = jnp.bfloat16
ANY = pl.BlockSpec(memory_space=pl.ANY)
SMEM = pl.BlockSpec(memory_space=pltpu.SMEM)
VMEM = pl.BlockSpec(memory_space=pltpu.VMEM)


def params(mib=60):
    return pltpu.CompilerParams(vmem_limit_bytes=mib << 20)


def cost(microseconds):
    return pl.CostEstimate(
        flops=microseconds * 1_000_000_000, bytes_accessed=1_000_000, transcendentals=0
    )


def run_copies(copies):
    for copy in copies:
        copy.start()
    for copy in copies:
        copy.wait()


def prep_kernel(head_size, roles, first_in, second_in, *refs):
    count = PLANE * len(CHUNKS)
    outs = refs[:count]
    rows, turned, in_sems, sems = refs[count:]
    loads = [
        pltpu.make_async_copy(ref, rows.at[index], in_sems.at[index])
        for index, ref in enumerate((first_in, second_in))
    ]
    for load in loads:
        load.start()
    for index, load in enumerate(loads):
        load.wait()
        turned[index] = rows[index].T
    place = roles[0]
    copies = []
    per_device = HEADS // PLANE
    first = 0
    for chunk, heads in enumerate(CHUNKS):
        for hop in range(PLANE):
            group = place ^ hop
            row = pl.multiple_of((group * per_device + first) * head_size, 16)
            number = chunk * PLANE + hop
            copies.append(
                pltpu.make_async_copy(
                    turned.at[:, pl.ds(row, heads * head_size)], outs[number], sems.at[number]
                )
            )
        first += heads
    run_copies(copies)


def limits_kernel(roles, local_blocks, far_blocks, counts, out):
    blocks = counts.shape[0]
    first = roles[1] * (PLANE * 2)
    for query in range(PLANE * 2):
        listed = [local_blocks[first + query, s] for s in range(local_blocks.shape[1])]
        listed += [far_blocks[first + query, s] for s in range(far_blocks.shape[1])]
        for slot in range(WINDOW * 2):
            key = first - 2 * FAR_UP + (query // 2) * 2 + slot
            found = listed[0] == key
            for entry in listed[1:]:
                found = found | (entry == key)
            inside = (key >= 0) & (key < blocks)
            count = counts[jnp.clip(key, 0, blocks - 1)]
            out[query * WINDOW * 2 + slot] = jnp.where(found & inside, count, 0)


def pack_kernel(roles, *refs):
    pieces = refs[:PLANE]
    even, odd = refs[PLANE : PLANE + 2]
    plane, sems = refs[PLANE + 2 :]
    place, parity = roles[0], roles[2]
    run_copies(
        [
            pltpu.make_async_copy(
                pieces[hop], plane.at[place ^ hop], sems.at[hop]
            )
            for hop in range(PLANE)
        ]
    )
    run_copies(
        [
            pltpu.make_async_copy(plane.at[pl.ds(2 - 2 * parity, 2)], even, sems.at[0]),
            pltpu.make_async_copy(plane.at[pl.ds(2 * parity, 2)], odd, sems.at[1]),
        ]
    )


def dot(a, b, left, right):
    return lax.dot_general(a, b, (((left,), (right,)), ((), ())), preferred_element_type=F32)


def main_kernel(head_size, heads, roles, limits, *refs):
    key_pieces = refs[:PLANE]
    query_pieces = refs[PLANE : 2 * PLANE]
    even_in, odd_in = refs[2 * PLANE : 2 * PLANE + 2]
    rest = refs[2 * PLANE + 2 :]
    outs = rest[:PLANE]
    local_out, even_out, odd_out = rest[PLANE : PLANE + 3]
    chain, query, result, key_sums, sums = rest[PLANE + 3 : PLANE + 8]
    scores, grads, peaks, weights, sems = (
        rest[PLANE + 8 : PLANE + 10],
        rest[PLANE + 10 : PLANE + 12],
        rest[PLANE + 12 : PLANE + 14],
        rest[PLANE + 14],
        rest[PLANE + 15],
    )
    place, parity = roles[0], roles[2]
    copies = []
    for hop in range(PLANE):
        unit = place ^ hop
        copies.append(
            pltpu.make_async_copy(key_pieces[hop], chain.at[FAR_UP + unit], sems.at[2 * hop])
        )
        copies.append(
            pltpu.make_async_copy(query_pieces[hop], query.at[unit], sems.at[2 * hop + 1])
        )
    above = FAR_UP + PLANE
    copies.append(
        pltpu.make_async_copy(
            even_in, chain.at[pl.ds((1 - parity) * above, 2)], sems.at[2 * PLANE]
        )
    )
    copies.append(
        pltpu.make_async_copy(odd_in, chain.at[pl.ds(parity * above, 2)], sems.at[2 * PLANE + 1])
    )
    for copy in copies:
        copy.start()
    key_sums[...] = jnp.zeros_like(key_sums)
    for copy in copies:
        copy.wait()

    scale = 1.0 / math.sqrt(head_size)
    rate = scale * math.log2(math.e)
    tokens = 2 * BLK
    row = lax.broadcasted_iota(jnp.int32, (BLK, tokens), 0)
    lane = lax.broadcasted_iota(jnp.int32, (1, tokens), 1)
    steps = heads * PLANE

    def score(index, slot, k, peak):
        head, unit = index // PLANE, index % PLANE
        tile = dot(chain[unit + k, 0, head], query[unit, 0, head], 0, 0)
        for half in range(2):
            place_in = 2 * k + half
            base = unit * 2 * WINDOW * 2 + place_in
            limit = jnp.where(lane < BLK, limits[base], limits[base + WINDOW * 2])
            part = jnp.where(row < limit, tile[half * BLK : (half + 1) * BLK], -1e30)
            top = jnp.max(part.reshape(BLK // 8, 8, tokens), axis=0)
            peak = top if peak is None else jnp.maximum(peak, top)
            scores[slot][place_in * BLK : (place_in + 1) * BLK] = part
        return peak

    def keep_peak(slot, peak):
        peak = jnp.max(peak, axis=0, keepdims=True)
        peaks[slot][...] = jnp.broadcast_to(peak, (8, tokens))

    def grad(index, slot, k):
        head, unit = index // PLANE, index % PLANE
        grads[slot][k * tokens : (k + 1) * tokens] = dot(
            chain[unit + k, 1, head], query[unit, 1, head], 0, 0
        )

    def step(index, now, later):
        head, unit = index // PLANE, index % PLANE
        after = jnp.minimum(index + 1, steps - 1)
        query_t = query[unit, 0, head]
        grad_wide = query[unit, 1, head].astype(F32)
        peak = peaks[now][0:1]
        total = out_t = later_peak = query_grad = None
        for k in range(WINDOW):
            span = slice(k * tokens, (k + 1) * tokens)
            power = jnp.exp2((scores[now][span] - peak) * rate)
            part = jnp.sum(power.reshape(tokens // 8, 8, tokens), axis=0)
            total = part if k == 0 else total + part
            weight = power.astype(BF16)
            weights[span] = weight
            part = dot(chain[unit + k, 1, head], weight, 1, 0)
            out_t = part if k == 0 else out_t + part
            later_peak = score(after, later, k, later_peak)
        keep_peak(later, later_peak)
        inverse = 1.0 / jnp.sum(total, axis=0, keepdims=True)
        attended = (out_t * inverse).astype(BF16)
        delta = jnp.sum(grad_wide * attended.astype(F32), axis=0, keepdims=True)
        grad_scaled = (grad_wide * inverse).astype(BF16)
        query_scaled = (query_t.astype(F32) * inverse).astype(BF16)
        for k in range(WINDOW):
            span = slice(k * tokens, (k + 1) * tokens)
            weight = weights[span]
            grad_scores = weight * (grads[now][span] - delta).astype(BF16)
            part = dot(chain[unit + k, 0, head], grad_scores, 1, 0)
            query_grad = part if k == 0 else query_grad + part
            key_sums[unit + k, 0, head] += dot(query_scaled, grad_scores, 1, 1)
            key_sums[unit + k, 1, head] += dot(grad_scaled, weight, 1, 1)
            grad(after, later, k)
        result[unit, 0, head] = attended
        result[unit, 1, head] = (query_grad * (inverse * scale)).astype(BF16)

    first_peak = None
    for k in range(WINDOW):
        first_peak = score(0, 0, k, first_peak)
        grad(0, 0, k)
    keep_peak(0, first_peak)

    def two_steps(index, carry):
        step(2 * index, 0, 1)
        step(2 * index + 1, 1, 0)
        return carry

    lax.fori_loop(0, steps // 2, two_steps, 0)
    copies = [
        pltpu.make_async_copy(result.at[place ^ hop], outs[hop], sems.at[hop])
        for hop in range(PLANE)
    ]
    for copy in copies:
        copy.start()
    for unit in range(CHAIN + 1):
        sums[unit, 0] = (key_sums[unit, 0] * scale).astype(BF16)
        sums[unit, 1] = key_sums[unit, 1].astype(BF16)
    more = [
        pltpu.make_async_copy(sums.at[pl.ds(FAR_UP, PLANE)], local_out, sems.at[PLANE]),
        pltpu.make_async_copy(
            sums.at[pl.ds((1 - parity) * above, 2)], even_out, sems.at[PLANE + 1]
        ),
        pltpu.make_async_copy(sums.at[pl.ds(parity * above, 2)], odd_out, sems.at[PLANE + 2]),
    ]
    for copy in more:
        copy.start()
    for copy in copies + more:
        copy.wait()


def join_kernel(roles, local, even_in, odd_in, *refs):
    outs = refs[:PLANE]
    held, sems = refs[PLANE:]
    place, parity = roles[0], roles[2]
    below_ok, above_ok = roles[3], roles[4]
    held[...] = local[...]

    def take(below, above):
        @pl.when(below_ok == 1)
        def _():
            held[0] = (held[0].astype(F32) + below[0].astype(F32)).astype(BF16)

        @pl.when(above_ok == 1)
        def _():
            for unit in range(2):
                held[2 + unit] = (held[2 + unit].astype(F32) + above[unit].astype(F32)).astype(
                    BF16
                )

    @pl.when(parity == 0)
    def _():
        take(odd_in, even_in)

    @pl.when(parity == 1)
    def _():
        take(even_in, odd_in)

    run_copies(
        [
            pltpu.make_async_copy(held.at[place ^ hop], outs[hop], sems.at[hop])
            for hop in range(PLANE)
        ]
    )


def finish_kernel(head_size, roles, *refs):
    count = PLANE * len(CHUNKS)
    pieces = refs[:count]
    first_out, second_out, turned, sems = refs[count:]
    place = roles[0]
    per_device = HEADS // PLANE
    copies = []
    first = 0
    for chunk, heads in enumerate(CHUNKS):
        for hop in range(PLANE):
            group = place ^ hop
            row = pl.multiple_of((group * per_device + first) * head_size, 16)
            number = chunk * PLANE + hop
            copies.append(
                pltpu.make_async_copy(
                    pieces[number], turned.at[:, pl.ds(row, heads * head_size)], sems.at[number]
                )
            )
        first += heads
    run_copies(copies)
    first_out[...] = turned[0].T
    second_out[...] = turned[1].T


def body(queries, keys, values, cotangent, local_blocks, far_blocks, counts):
    tokens, width = queries.shape
    head_size = width // HEADS
    size = lax.axis_size("seq")
    planes = size // PLANE
    device = lax.axis_index("seq")
    level = device // PLANE
    roles = jnp.stack(
        [
            device % PLANE,
            level,
            level % 2,
            (level > 0).astype(jnp.int32),
            (level < planes - 1).astype(jnp.int32),
        ]
    ).astype(jnp.int32)

    def swap(array, hop):
        pairs = [(i, (i // PLANE) * PLANE + ((i % PLANE) ^ hop)) for i in range(size)]
        return lax.ppermute(array, "seq", pairs)

    def level_swap(array, odd):
        pairs = []
        for i in range(size):
            z = i // PLANE
            other = z + 1 if z % 2 == odd else z - 1
            pairs.append((i, i + (other - z) * PLANE if 0 <= other < planes else i))
        return lax.ppermute(array, "seq", pairs)

    def piece(heads):
        return jax.ShapeDtypeStruct((2, heads * head_size, tokens), BF16)

    def prep(first, second):
        return pl.pallas_call(
            lambda *refs: prep_kernel(head_size, *refs),
            out_shape=[piece(heads) for heads in CHUNKS for _ in range(PLANE)],
            in_specs=[SMEM, ANY, ANY],
            out_specs=[ANY] * (PLANE * len(CHUNKS)),
            scratch_shapes=[
                pltpu.VMEM((2, tokens, width), BF16),
                pltpu.VMEM((2, width, tokens), BF16),
                pltpu.SemaphoreType.DMA((2,)),
                pltpu.SemaphoreType.DMA((PLANE * len(CHUNKS),)),
            ],
            compiler_params=params(),
            cost_estimate=cost(3),
        )(roles, first, second)

    def spread(parts):
        return [
            [parts[chunk * PLANE]]
            + [swap(parts[chunk * PLANE + hop], hop) for hop in range(1, PLANE)]
            for chunk in range(len(CHUNKS))
        ]

    key_held = spread(prep(keys, values))
    query_held = spread(prep(queries, cotangent))
    limits = pl.pallas_call(
        limits_kernel,
        out_shape=jax.ShapeDtypeStruct((PLANE * 2 * WINDOW * 2,), jnp.int32),
        in_specs=[SMEM] * 4,
        out_specs=SMEM,
    )(roles, local_blocks, far_blocks, counts)

    query_pieces = []
    key_pieces = []
    halos = []
    for chunk, heads in enumerate(CHUNKS):
        held = key_held[chunk]
        pair = jax.ShapeDtypeStruct((2, 2, heads * head_size, tokens), BF16)
        even, odd = pl.pallas_call(
            pack_kernel,
            out_shape=[pair, pair],
            in_specs=[SMEM] + [ANY] * PLANE,
            out_specs=[ANY, ANY],
            scratch_shapes=[
                pltpu.VMEM((PLANE, 2, heads * head_size, tokens), BF16),
                pltpu.SemaphoreType.DMA((PLANE,)),
            ],
            compiler_params=params(),
        )(roles, *held)
        halos.append((level_swap(even, 0), level_swap(odd, 1)))

    for chunk, heads in enumerate(CHUNKS):
        even, odd = halos[chunk]
        shape = (heads, head_size, tokens)
        results = pl.pallas_call(
            lambda *refs, heads=heads: main_kernel(head_size, heads, *refs),
            out_shape=[jax.ShapeDtypeStruct((2,) + shape, BF16)] * PLANE
            + [jax.ShapeDtypeStruct((PLANE, 2) + shape, BF16)]
            + [jax.ShapeDtypeStruct((2, 2) + shape, BF16)] * 2,
            in_specs=[SMEM, SMEM] + [ANY] * (2 * PLANE + 2),
            out_specs=[ANY] * (PLANE + 3),
            scratch_shapes=[
                pltpu.VMEM((CHAIN + 1, 2) + shape, BF16),
                pltpu.VMEM((PLANE, 2) + shape, BF16),
                pltpu.VMEM((PLANE, 2) + shape, BF16),
                pltpu.VMEM((CHAIN + 1, 2) + shape, F32),
                pltpu.VMEM((CHAIN + 1, 2) + shape, BF16),
                pltpu.VMEM((WINDOW * tokens, tokens), F32),
                pltpu.VMEM((WINDOW * tokens, tokens), F32),
                pltpu.VMEM((WINDOW * tokens, tokens), F32),
                pltpu.VMEM((WINDOW * tokens, tokens), F32),
                pltpu.VMEM((8, tokens), F32),
                pltpu.VMEM((8, tokens), F32),
                pltpu.VMEM((WINDOW * tokens, tokens), BF16),
                pltpu.SemaphoreType.DMA((2 * PLANE + 2,)),
            ],
            compiler_params=params(),
            cost_estimate=cost(6 * heads),
        )(
            roles,
            limits,
            *[part.reshape((2,) + shape) for part in key_held[chunk] + query_held[chunk]],
            even.reshape((2, 2) + shape),
            odd.reshape((2, 2) + shape),
        )
        flat = (2, heads * head_size, tokens)
        out = [part.reshape(flat) for part in results[:PLANE]]
        query_pieces += [out[0]] + [swap(out[hop], hop) for hop in range(1, PLANE)]
        local, even, odd = results[PLANE:]
        even, odd = level_swap(even, 0), level_swap(odd, 1)
        back = pl.pallas_call(
            join_kernel,
            out_shape=[piece(heads)] * PLANE,
            in_specs=[SMEM] + [VMEM] * 3,
            out_specs=[ANY] * PLANE,
            scratch_shapes=[
                pltpu.VMEM((PLANE,) + flat, BF16),
                pltpu.SemaphoreType.DMA((PLANE,)),
            ],
            compiler_params=params(),
        )(roles, local.reshape((PLANE,) + flat), even.reshape((2,) + flat), odd.reshape((2,) + flat))
        key_pieces += [back[0]] + [swap(back[hop], hop) for hop in range(1, PLANE)]

    def finish(parts):
        return pl.pallas_call(
            lambda *refs: finish_kernel(head_size, *refs),
            out_shape=[jax.ShapeDtypeStruct((tokens, width), BF16)] * 2,
            in_specs=[SMEM] + [ANY] * len(parts),
            out_specs=[VMEM, VMEM],
            scratch_shapes=[
                pltpu.VMEM((2, width, tokens), BF16),
                pltpu.SemaphoreType.DMA((len(parts),)),
            ],
            compiler_params=params(),
        )(roles, *parts)

    attended, query_grad = finish(query_pieces)
    key_grad, value_grad = finish(key_pieces)
    return attended, query_grad, key_grad, value_grad


def solution(mesh):
    rows = P(("groups", "seq"), None)
    return jax.shard_map(
        body,
        mesh=mesh,
        in_specs=(rows, rows, rows, rows, P("groups", None), P("groups", None), P("groups")),
        out_specs=(rows, rows, rows, rows),
        check_vma=False,
    )
```

```python
import math

import jax
import jax.numpy as jnp
from jax import lax
from jax.experimental import pallas as pl
from jax.experimental.pallas import tpu as pltpu
from jax.sharding import PartitionSpec as P

HEADS = 16
BLK = 128
PLANE = 4
CHUNKS = (2, 2)
FAR_UP = 2
WINDOW = 4
CHAIN = PLANE + FAR_UP + 1
F32 = jnp.float32
BF16 = jnp.bfloat16
ANY = pl.BlockSpec(memory_space=pl.ANY)
SMEM = pl.BlockSpec(memory_space=pltpu.SMEM)
VMEM = pl.BlockSpec(memory_space=pltpu.VMEM)


def params(mib=60):
    return pltpu.CompilerParams(vmem_limit_bytes=mib << 20)


def after(arrays, others):
    return list(lax.optimization_barrier((list(arrays), list(others)))[0])


def cost(microseconds):
    return pl.CostEstimate(
        flops=microseconds * 1_000_000_000, bytes_accessed=1_000_000, transcendentals=0
    )


def run_copies(copies):
    for copy in copies:
        copy.start()
    for copy in copies:
        copy.wait()


def prep_kernel(head_size, roles, first_in, second_in, *refs):
    count = PLANE * len(CHUNKS)
    outs = refs[:count]
    rows, turned, in_sems, sems = refs[count:]
    loads = [
        pltpu.make_async_copy(ref, rows.at[index], in_sems.at[index])
        for index, ref in enumerate((first_in, second_in))
    ]
    for load in loads:
        load.start()
    for index, load in enumerate(loads):
        load.wait()
        turned[index] = rows[index].T
    place = roles[0]
    copies = []
    per_device = HEADS // PLANE
    first = 0
    for chunk, heads in enumerate(CHUNKS):
        for hop in range(PLANE):
            group = place ^ hop
            row = pl.multiple_of((group * per_device + first) * head_size, 16)
            number = chunk * PLANE + hop
            copies.append(
                pltpu.make_async_copy(
                    turned.at[:, pl.ds(row, heads * head_size)], outs[number], sems.at[number]
                )
            )
        first += heads
    run_copies(copies)


def limits_kernel(roles, local_blocks, far_blocks, counts, out):
    blocks = counts.shape[0]
    first = roles[1] * (PLANE * 2)
    for query in range(PLANE * 2):
        listed = [local_blocks[first + query, s] for s in range(local_blocks.shape[1])]
        listed += [far_blocks[first + query, s] for s in range(far_blocks.shape[1])]
        for slot in range(WINDOW * 2):
            key = first - 2 * FAR_UP + (query // 2) * 2 + slot
            found = listed[0] == key
            for entry in listed[1:]:
                found = found | (entry == key)
            inside = (key >= 0) & (key < blocks)
            count = counts[jnp.clip(key, 0, blocks - 1)]
            out[query * WINDOW * 2 + slot] = jnp.where(found & inside, count, 0)


def pack_kernel(roles, *refs):
    pieces = refs[:PLANE]
    even, odd = refs[PLANE : PLANE + 2]
    plane, sems = refs[PLANE + 2 :]
    place, parity = roles[0], roles[2]
    run_copies(
        [
            pltpu.make_async_copy(pieces[hop], plane.at[place ^ hop], sems.at[hop])
            for hop in range(PLANE)
        ]
    )
    run_copies(
        [
            pltpu.make_async_copy(plane.at[pl.ds(2 - 2 * parity, 2)], even, sems.at[0]),
            pltpu.make_async_copy(plane.at[pl.ds(2 * parity, 2)], odd, sems.at[1]),
        ]
    )


def dot(a, b, left, right):
    return lax.dot_general(a, b, (((left,), (right,)), ((), ())), preferred_element_type=F32)


def main_kernel(head_size, heads, roles, limits, *refs):
    key_pieces = refs[:PLANE]
    query_pieces = refs[PLANE : 2 * PLANE]
    even_in, odd_in = refs[2 * PLANE : 2 * PLANE + 2]
    rest = refs[2 * PLANE + 2 :]
    outs = rest[:PLANE]
    local_out, even_out, odd_out = rest[PLANE : PLANE + 3]
    chain, query, result, key_sums, sums = rest[PLANE + 3 : PLANE + 8]
    scores, grads, peaks, weights, sems = (
        rest[PLANE + 8 : PLANE + 10],
        rest[PLANE + 10 : PLANE + 12],
        rest[PLANE + 12 : PLANE + 14],
        rest[PLANE + 14],
        rest[PLANE + 15],
    )
    place, parity = roles[0], roles[2]
    copies = []
    for hop in range(PLANE):
        unit = place ^ hop
        copies.append(
            pltpu.make_async_copy(key_pieces[hop], chain.at[FAR_UP + unit], sems.at[2 * hop])
        )
        copies.append(
            pltpu.make_async_copy(query_pieces[hop], query.at[unit], sems.at[2 * hop + 1])
        )
    above = FAR_UP + PLANE
    copies.append(
        pltpu.make_async_copy(
            even_in, chain.at[pl.ds((1 - parity) * above, 2)], sems.at[2 * PLANE]
        )
    )
    copies.append(
        pltpu.make_async_copy(odd_in, chain.at[pl.ds(parity * above, 2)], sems.at[2 * PLANE + 1])
    )
    for copy in copies:
        copy.start()
    key_sums[...] = jnp.zeros_like(key_sums)
    for copy in copies:
        copy.wait()

    scale = 1.0 / math.sqrt(head_size)
    rate = scale * math.log2(math.e)
    tokens = 2 * BLK
    row = lax.broadcasted_iota(jnp.int32, (BLK, tokens), 0)
    lane = lax.broadcasted_iota(jnp.int32, (1, tokens), 1)
    steps = heads * PLANE

    def score(index, slot, k, peak):
        head, unit = index // PLANE, index % PLANE
        tile = dot(chain[unit + k, 0, head], query[unit, 0, head], 0, 0)
        for half in range(2):
            place_in = 2 * k + half
            base = unit * 2 * WINDOW * 2 + place_in
            limit = jnp.where(lane < BLK, limits[base], limits[base + WINDOW * 2])
            part = jnp.where(row < limit, tile[half * BLK : (half + 1) * BLK], -1e30)
            top = jnp.max(part.reshape(BLK // 8, 8, tokens), axis=0)
            peak = top if peak is None else jnp.maximum(peak, top)
            scores[slot][place_in * BLK : (place_in + 1) * BLK] = part
        return peak

    def keep_peak(slot, peak):
        peak = jnp.max(peak, axis=0, keepdims=True)
        peaks[slot][...] = jnp.broadcast_to(peak, (8, tokens))

    def grad(index, slot, k):
        head, unit = index // PLANE, index % PLANE
        grads[slot][k * tokens : (k + 1) * tokens] = dot(
            chain[unit + k, 1, head], query[unit, 1, head], 0, 0
        )

    def step(index, now, later):
        head, unit = index // PLANE, index % PLANE
        after = jnp.minimum(index + 1, steps - 1)
        query_t = query[unit, 0, head]
        grad_wide = query[unit, 1, head].astype(F32)
        peak = peaks[now][0:1]
        total = out_t = later_peak = query_grad = None
        for k in range(WINDOW):
            span = slice(k * tokens, (k + 1) * tokens)
            power = jnp.exp2((scores[now][span] - peak) * rate)
            part = jnp.sum(power.reshape(tokens // 8, 8, tokens), axis=0)
            total = part if k == 0 else total + part
            weight = power.astype(BF16)
            weights[span] = weight
            part = dot(chain[unit + k, 1, head], weight, 1, 0)
            out_t = part if k == 0 else out_t + part
            later_peak = score(after, later, k, later_peak)
        keep_peak(later, later_peak)
        inverse = 1.0 / jnp.sum(total, axis=0, keepdims=True)
        attended = (out_t * inverse).astype(BF16)
        delta = jnp.sum(grad_wide * attended.astype(F32), axis=0, keepdims=True)
        grad_scaled = (grad_wide * inverse).astype(BF16)
        query_scaled = (query_t.astype(F32) * inverse).astype(BF16)
        for k in range(WINDOW):
            span = slice(k * tokens, (k + 1) * tokens)
            weight = weights[span]
            grad_scores = weight * (grads[now][span] - delta).astype(BF16)
            part = dot(chain[unit + k, 0, head], grad_scores, 1, 0)
            query_grad = part if k == 0 else query_grad + part
            key_sums[unit + k, 0, head] += dot(query_scaled, grad_scores, 1, 1)
            key_sums[unit + k, 1, head] += dot(grad_scaled, weight, 1, 1)
            grad(after, later, k)
        result[unit, 0, head] = attended
        result[unit, 1, head] = (query_grad * (inverse * scale)).astype(BF16)

    first_peak = None
    for k in range(WINDOW):
        first_peak = score(0, 0, k, first_peak)
        grad(0, 0, k)
    keep_peak(0, first_peak)

    def two_steps(index, carry):
        step(2 * index, 0, 1)
        step(2 * index + 1, 1, 0)
        return carry

    lax.fori_loop(0, steps // 2, two_steps, 0)
    copies = [
        pltpu.make_async_copy(result.at[place ^ hop], outs[hop], sems.at[hop])
        for hop in range(PLANE)
    ]
    for copy in copies:
        copy.start()
    for unit in range(CHAIN + 1):
        sums[unit, 0] = (key_sums[unit, 0] * scale).astype(BF16)
        sums[unit, 1] = key_sums[unit, 1].astype(BF16)
    more = [
        pltpu.make_async_copy(sums.at[pl.ds(FAR_UP, PLANE)], local_out, sems.at[PLANE]),
        pltpu.make_async_copy(
            sums.at[pl.ds((1 - parity) * above, 2)], even_out, sems.at[PLANE + 1]
        ),
        pltpu.make_async_copy(sums.at[pl.ds(parity * above, 2)], odd_out, sems.at[PLANE + 2]),
    ]
    for copy in more:
        copy.start()
    for copy in copies + more:
        copy.wait()


def join_kernel(roles, local, even_in, odd_in, *refs):
    outs = refs[:PLANE]
    held, sems = refs[PLANE:]
    place, parity = roles[0], roles[2]
    below_ok, above_ok = roles[3], roles[4]
    held[...] = local[...]

    def take(below, above):
        @pl.when(below_ok == 1)
        def _():
            held[0] = (held[0].astype(F32) + below[0].astype(F32)).astype(BF16)

        @pl.when(above_ok == 1)
        def _():
            for unit in range(2):
                held[2 + unit] = (held[2 + unit].astype(F32) + above[unit].astype(F32)).astype(
                    BF16
                )

    @pl.when(parity == 0)
    def _():
        take(odd_in, even_in)

    @pl.when(parity == 1)
    def _():
        take(even_in, odd_in)

    run_copies(
        [
            pltpu.make_async_copy(held.at[place ^ hop], outs[hop], sems.at[hop])
            for hop in range(PLANE)
        ]
    )


def finish_kernel(head_size, roles, *refs):
    count = PLANE * len(CHUNKS)
    pieces = refs[:count]
    first_out, second_out, turned, sems = refs[count:]
    place = roles[0]
    per_device = HEADS // PLANE
    copies = []
    first = 0
    for chunk, heads in enumerate(CHUNKS):
        for hop in range(PLANE):
            group = place ^ hop
            row = pl.multiple_of((group * per_device + first) * head_size, 16)
            number = chunk * PLANE + hop
            copies.append(
                pltpu.make_async_copy(
                    pieces[number], turned.at[:, pl.ds(row, heads * head_size)], sems.at[number]
                )
            )
        first += heads
    run_copies(copies)
    first_out[...] = turned[0].T
    second_out[...] = turned[1].T


def body(queries, keys, values, cotangent, local_blocks, far_blocks, counts):
    tokens, width = queries.shape
    head_size = width // HEADS
    size = lax.axis_size("seq")
    planes = size // PLANE
    device = lax.axis_index("seq")
    level = device // PLANE
    roles = jnp.stack(
        [
            device % PLANE,
            level,
            level % 2,
            (level > 0).astype(jnp.int32),
            (level < planes - 1).astype(jnp.int32),
        ]
    ).astype(jnp.int32)

    def swap(array, hop):
        pairs = [(i, (i // PLANE) * PLANE + ((i % PLANE) ^ hop)) for i in range(size)]
        return lax.ppermute(array, "seq", pairs)

    def level_swap(array, odd):
        pairs = []
        for i in range(size):
            z = i // PLANE
            other = z + 1 if z % 2 == odd else z - 1
            pairs.append((i, i + (other - z) * PLANE if 0 <= other < planes else i ^ 1))
        return lax.ppermute(array, "seq", pairs)

    def piece(heads):
        return jax.ShapeDtypeStruct((2, heads * head_size, tokens), BF16)

    def prep(first, second):
        return pl.pallas_call(
            lambda *refs: prep_kernel(head_size, *refs),
            out_shape=[piece(heads) for heads in CHUNKS for _ in range(PLANE)],
            in_specs=[SMEM, ANY, ANY],
            out_specs=[ANY] * (PLANE * len(CHUNKS)),
            scratch_shapes=[
                pltpu.VMEM((2, tokens, width), BF16),
                pltpu.VMEM((2, width, tokens), BF16),
                pltpu.SemaphoreType.DMA((2,)),
                pltpu.SemaphoreType.DMA((PLANE * len(CHUNKS),)),
            ],
            compiler_params=params(),
            cost_estimate=cost(3),
        )(roles, first, second)

    def spread(parts):
        return [
            [parts[chunk * PLANE]]
            + [swap(parts[chunk * PLANE + hop], hop) for hop in range(1, PLANE)]
            for chunk in range(len(CHUNKS))
        ]

    key_held = spread(prep(keys, values))
    limits = pl.pallas_call(
        limits_kernel,
        out_shape=jax.ShapeDtypeStruct((PLANE * 2 * WINDOW * 2,), jnp.int32),
        in_specs=[SMEM] * 4,
        out_specs=SMEM,
    )(roles, local_blocks, far_blocks, counts)

    query_pieces = []
    key_pieces = []
    halos = []
    query_ready = prep(queries, cotangent)
    query_held = spread(query_ready)
    for chunk, heads in enumerate(CHUNKS):
        held = key_held[chunk]
        held = after(held, query_held[0][1:] if chunk else query_ready)
        pair = jax.ShapeDtypeStruct((2, 2, heads * head_size, tokens), BF16)
        even, odd = pl.pallas_call(
            pack_kernel,
            out_shape=[pair, pair],
            in_specs=[SMEM] + [ANY] * PLANE,
            out_specs=[ANY, ANY],
            scratch_shapes=[
                pltpu.VMEM((PLANE, 2, heads * head_size, tokens), BF16),
                pltpu.SemaphoreType.DMA((PLANE,)),
            ],
            compiler_params=params(),
            cost_estimate=cost(2),
        )(roles, *held)
        halos.append((level_swap(even, 0), level_swap(odd, 1)))

    def main(chunk):
        heads = CHUNKS[chunk]
        even, odd = halos[chunk]
        shape = (heads, head_size, tokens)
        return pl.pallas_call(
            lambda *refs: main_kernel(head_size, heads, *refs),
            out_shape=[jax.ShapeDtypeStruct((2,) + shape, BF16)] * PLANE
            + [jax.ShapeDtypeStruct((PLANE, 2) + shape, BF16)]
            + [jax.ShapeDtypeStruct((2, 2) + shape, BF16)] * 2,
            in_specs=[SMEM, SMEM] + [ANY] * (2 * PLANE + 2),
            out_specs=[ANY] * (PLANE + 3),
            scratch_shapes=[
                pltpu.VMEM((CHAIN + 1, 2) + shape, BF16),
                pltpu.VMEM((PLANE, 2) + shape, BF16),
                pltpu.VMEM((PLANE, 2) + shape, BF16),
                pltpu.VMEM((CHAIN + 1, 2) + shape, F32),
                pltpu.VMEM((CHAIN + 1, 2) + shape, BF16),
                pltpu.VMEM((WINDOW * tokens, tokens), F32),
                pltpu.VMEM((WINDOW * tokens, tokens), F32),
                pltpu.VMEM((WINDOW * tokens, tokens), F32),
                pltpu.VMEM((WINDOW * tokens, tokens), F32),
                pltpu.VMEM((8, tokens), F32),
                pltpu.VMEM((8, tokens), F32),
                pltpu.VMEM((WINDOW * tokens, tokens), BF16),
                pltpu.SemaphoreType.DMA((2 * PLANE + 2,)),
            ],
            compiler_params=params(),
            cost_estimate=cost(6 * heads),
        )(
            roles,
            limits,
            *[part.reshape((2,) + shape) for part in key_held[chunk] + query_held[chunk]],
            even.reshape((2, 2) + shape),
            odd.reshape((2, 2) + shape),
        )

    def join(chunk, local, even, odd):
        heads = CHUNKS[chunk]
        flat = (2, heads * head_size, tokens)
        return pl.pallas_call(
            join_kernel,
            out_shape=[piece(heads)] * PLANE,
            in_specs=[SMEM] + [VMEM] * 3,
            out_specs=[ANY] * PLANE,
            scratch_shapes=[
                pltpu.VMEM((PLANE,) + flat, BF16),
                pltpu.SemaphoreType.DMA((PLANE,)),
            ],
            compiler_params=params(),
        )(roles, local.reshape((PLANE,) + flat), even.reshape((2,) + flat), odd.reshape((2,) + flat))

    def spread_one(parts):
        return [parts[0]] + [swap(parts[hop], hop) for hop in range(1, PLANE)]

    rounds = len(CHUNKS)
    results = [main(chunk) for chunk in range(rounds)]
    backs = []
    last = None
    for chunk in range(rounds):
        shape = (2, CHUNKS[chunk] * head_size, tokens)
        out = [part.reshape(shape) for part in results[chunk][:PLANE]]
        if last is not None:
            out = after(out, last[1:])
        last = spread_one(out)
        query_pieces += last
    for chunk in range(rounds):
        local, even, odd = results[chunk][PLANE:]
        back = join(chunk, local, level_swap(even, 0), level_swap(odd, 1))
        back = after(back, [last[2]])
        last = spread_one(back)
        key_pieces += last

    def finish(parts):
        return pl.pallas_call(
            lambda *refs: finish_kernel(head_size, *refs),
            out_shape=[jax.ShapeDtypeStruct((tokens, width), BF16)] * 2,
            in_specs=[SMEM] + [ANY] * len(parts),
            out_specs=[VMEM, VMEM],
            scratch_shapes=[
                pltpu.VMEM((2, width, tokens), BF16),
                pltpu.SemaphoreType.DMA((len(parts),)),
            ],
            compiler_params=params(),
        )(roles, *parts)

    attended, query_grad = finish(query_pieces)
    key_grad, value_grad = finish(key_pieces)
    return attended, query_grad, key_grad, value_grad


def solution(mesh):
    rows = P(("groups", "seq"), None)
    return jax.shard_map(
        body,
        mesh=mesh,
        in_specs=(rows, rows, rows, rows, P("groups", None), P("groups", None), P("groups")),
        out_specs=(rows, rows, rows, rows),
        check_vma=False,
    )
```

```python
import math

import jax
import jax.numpy as jnp
from jax import lax
from jax.experimental import pallas as pl
from jax.experimental.pallas import tpu as pltpu
from jax.sharding import PartitionSpec as P

HEADS = 16
BLK = 128
PLANE = 4
CHUNKS = (2, 2)
FAR_UP = 2
WINDOW = 4
CHAIN = PLANE + FAR_UP + 1
STRIP = 64
F32 = jnp.float32
BF16 = jnp.bfloat16
ANY = pl.BlockSpec(memory_space=pl.ANY)
SMEM = pl.BlockSpec(memory_space=pltpu.SMEM)
VMEM = pl.BlockSpec(memory_space=pltpu.VMEM)


def params(mib=60):
    return pltpu.CompilerParams(vmem_limit_bytes=mib << 20)


def after(arrays, others):
    return list(lax.optimization_barrier((list(arrays), list(others)))[0])


def cost(microseconds):
    return pl.CostEstimate(
        flops=microseconds * 1_000_000_000, bytes_accessed=1_000_000, transcendentals=0
    )


def run_copies(copies):
    for copy in copies:
        copy.start()
    for copy in copies:
        copy.wait()


def prep_kernel(head_size, lists, roles, first_in, second_in, *refs):
    count = PLANE * len(CHUNKS)
    lists_in, refs = refs[:lists], refs[lists:]
    outs = refs[:count]
    rows, turned, in_sems, sems = refs[-4:]
    loads = [
        pltpu.make_async_copy(ref, rows.at[index], in_sems.at[index])
        for index, ref in enumerate((first_in, second_in))
    ]
    for load in loads:
        load.start()
    if lists:
        find_limits(roles, *lists_in, refs[count])
    for index, load in enumerate(loads):
        load.wait()
        turned[index] = rows[index].T
    place = roles[0]
    copies = []
    per_device = HEADS // PLANE
    first = 0
    for chunk, heads in enumerate(CHUNKS):
        for hop in range(PLANE):
            group = place ^ hop
            row = pl.multiple_of((group * per_device + first) * head_size, 16)
            number = chunk * PLANE + hop
            copies.append(
                pltpu.make_async_copy(
                    turned.at[:, pl.ds(row, heads * head_size)], outs[number], sems.at[number]
                )
            )
        first += heads
    run_copies(copies)


def find_limits(roles, local_blocks, far_blocks, counts, out):
    blocks = counts.shape[0]
    first = roles[1] * (PLANE * 2)
    for query in range(PLANE * 2):
        listed = [local_blocks[first + query, s] for s in range(local_blocks.shape[1])]
        listed += [far_blocks[first + query, s] for s in range(far_blocks.shape[1])]
        for slot in range(WINDOW * 2):
            key = first - 2 * FAR_UP + (query // 2) * 2 + slot
            found = listed[0] == key
            for entry in listed[1:]:
                found = found | (entry == key)
            inside = (key >= 0) & (key < blocks)
            count = counts[jnp.clip(key, 0, blocks - 1)]
            out[query * WINDOW * 2 + slot] = jnp.where(found & inside, count, 0)


def pack_kernel(roles, *refs):
    pieces = refs[:PLANE]
    even, odd = refs[PLANE : PLANE + 2]
    plane, sems = refs[PLANE + 2 :]
    place, parity = roles[0], roles[2]
    run_copies(
        [
            pltpu.make_async_copy(pieces[hop], plane.at[place ^ hop], sems.at[hop])
            for hop in range(PLANE)
        ]
    )
    run_copies(
        [
            pltpu.make_async_copy(plane.at[pl.ds(2 - 2 * parity, 2)], even, sems.at[0]),
            pltpu.make_async_copy(plane.at[pl.ds(2 * parity, 2)], odd, sems.at[1]),
        ]
    )


def dot(a, b, left, right):
    return lax.dot_general(a, b, (((left,), (right,)), ((), ())), preferred_element_type=F32)


def main_kernel(head_size, heads, roles, limits, *refs):
    key_pieces = refs[:PLANE]
    query_pieces = refs[PLANE : 2 * PLANE]
    even_in, odd_in = refs[2 * PLANE : 2 * PLANE + 2]
    rest = refs[2 * PLANE + 2 :]
    outs = rest[:PLANE]
    local_out, even_out, odd_out = rest[PLANE : PLANE + 3]
    chain, query, result, key_sums, sums = rest[PLANE + 3 : PLANE + 8]
    scores, grads, peaks = (rest[PLANE + 8 + 2 * i : PLANE + 10 + 2 * i] for i in range(3))
    weights, grad_scores, sems = rest[PLANE + 14 :]
    place, parity = roles[0], roles[2]
    copies = []
    for hop in range(PLANE):
        unit = place ^ hop
        copies.append(
            pltpu.make_async_copy(key_pieces[hop], chain.at[FAR_UP + unit], sems.at[2 * hop])
        )
        copies.append(
            pltpu.make_async_copy(query_pieces[hop], query.at[unit], sems.at[2 * hop + 1])
        )
    above = FAR_UP + PLANE
    copies.append(
        pltpu.make_async_copy(
            even_in, chain.at[pl.ds((1 - parity) * above, 2)], sems.at[2 * PLANE]
        )
    )
    copies.append(
        pltpu.make_async_copy(odd_in, chain.at[pl.ds(parity * above, 2)], sems.at[2 * PLANE + 1])
    )
    for copy in copies:
        copy.start()
    key_sums[...] = jnp.zeros_like(key_sums)
    for copy in copies:
        copy.wait()

    scale = 1.0 / math.sqrt(head_size)
    rate = scale * math.log2(math.e)
    tokens = 2 * BLK
    row = lax.broadcasted_iota(jnp.int32, (BLK, tokens), 0)
    lane = lax.broadcasted_iota(jnp.int32, (1, tokens), 1)
    steps = heads * PLANE

    def score(index, slot, k, peak):
        head, unit = index // PLANE, index % PLANE
        tile = dot(chain[unit + k, 0, head], query[unit, 0, head], 0, 0)
        for half in range(2):
            block = 2 * k + half
            base = unit * 2 * WINDOW * 2 + block
            limit = jnp.where(lane < BLK, limits[base], limits[base + WINDOW * 2])
            for at in range(0, BLK, STRIP):
                part = tile[half * BLK + at : half * BLK + at + STRIP]
                part = jnp.where(row[at : at + STRIP] < limit, part, -1e30)
                top = jnp.max(part.reshape(STRIP // 8, 8, tokens), axis=0)
                peak = top if peak is None else jnp.maximum(peak, top)
                scores[slot][block * BLK + at : block * BLK + at + STRIP] = part
        return peak

    def keep_peak(slot, peak):
        peak = jnp.max(peak, axis=0, keepdims=True)
        peaks[slot][...] = jnp.broadcast_to(peak, (8, tokens))

    def grad(index, slot, k):
        head, unit = index // PLANE, index % PLANE
        grads[slot][k * tokens : (k + 1) * tokens] = dot(
            chain[unit + k, 1, head], query[unit, 1, head], 0, 0
        )

    def step(index, now, later, final=False):
        head, unit = index // PLANE, index % PLANE
        query_t = query[unit, 0, head]
        grad_wide = query[unit, 1, head].astype(F32)
        peak = peaks[now][0:1]
        total = out_t = later_peak = query_grad = None
        for k in range(WINDOW):
            span = slice(k * tokens, (k + 1) * tokens)
            if not final:
                later_peak = score(index + 1, later, k, later_peak)
            for at in range(k * tokens, (k + 1) * tokens, STRIP):
                power = jnp.exp2((scores[now][at : at + STRIP] - peak) * rate)
                part = jnp.sum(power.reshape(STRIP // 8, 8, tokens), axis=0)
                total = part if total is None else total + part
                weights[at : at + STRIP] = power.astype(BF16)
            part = dot(chain[unit + k, 1, head], weights[span], 1, 0)
            out_t = part if k == 0 else out_t + part
        if not final:
            keep_peak(later, later_peak)
        inverse = 1.0 / jnp.sum(total, axis=0, keepdims=True)
        attended = (out_t * inverse).astype(BF16)
        delta = jnp.sum(grad_wide * attended.astype(F32), axis=0, keepdims=True)
        grad_scaled = (grad_wide * inverse).astype(BF16)
        query_scaled = (query_t.astype(F32) * inverse).astype(BF16)
        for k in range(WINDOW):
            span = slice(k * tokens, (k + 1) * tokens)
            key_sums[unit + k, 1, head] += dot(grad_scaled, weights[span], 1, 1)
        for k in range(WINDOW):
            span = slice(k * tokens, (k + 1) * tokens)
            if not final:
                grad(index + 1, later, k)
            for at in range(k * tokens, (k + 1) * tokens, STRIP):
                change = (grads[now][at : at + STRIP] - delta).astype(BF16)
                grad_scores[at : at + STRIP] = weights[at : at + STRIP] * change
            part = dot(chain[unit + k, 0, head], grad_scores[span], 1, 0)
            query_grad = part if k == 0 else query_grad + part
            key_sums[unit + k, 0, head] += dot(query_scaled, grad_scores[span], 1, 1)
        result[unit, 0, head] = attended
        result[unit, 1, head] = (query_grad * (inverse * scale)).astype(BF16)

    first_peak = None
    for k in range(WINDOW):
        first_peak = score(0, 0, k, first_peak)
        grad(0, 0, k)
    keep_peak(0, first_peak)

    def two_steps(index, carry):
        step(2 * index, 0, 1)
        step(2 * index + 1, 1, 0)
        return carry

    lax.fori_loop(0, steps // 2 - 1, two_steps, 0)
    step(steps - 2, 0, 1)
    step(steps - 1, 1, 0, final=True)
    copies = [
        pltpu.make_async_copy(result.at[place ^ hop], outs[hop], sems.at[hop])
        for hop in range(PLANE)
    ]
    for copy in copies:
        copy.start()
    for unit in range(CHAIN + 1):
        sums[unit, 0] = (key_sums[unit, 0] * scale).astype(BF16)
        sums[unit, 1] = key_sums[unit, 1].astype(BF16)
    more = [
        pltpu.make_async_copy(sums.at[pl.ds(FAR_UP, PLANE)], local_out, sems.at[PLANE]),
        pltpu.make_async_copy(
            sums.at[pl.ds((1 - parity) * above, 2)], even_out, sems.at[PLANE + 1]
        ),
        pltpu.make_async_copy(sums.at[pl.ds(parity * above, 2)], odd_out, sems.at[PLANE + 2]),
    ]
    for copy in more:
        copy.start()
    for copy in copies + more:
        copy.wait()


def join_kernel(roles, local, even_in, odd_in, *refs):
    outs = refs[:PLANE]
    held, sems = refs[PLANE:]
    place, parity = roles[0], roles[2]
    below_ok, above_ok = roles[3], roles[4]
    held[...] = local[...]

    def take(below, above):
        @pl.when(below_ok == 1)
        def _():
            held[0] = (held[0].astype(F32) + below[0].astype(F32)).astype(BF16)

        @pl.when(above_ok == 1)
        def _():
            for unit in range(2):
                held[2 + unit] = (held[2 + unit].astype(F32) + above[unit].astype(F32)).astype(
                    BF16
                )

    @pl.when(parity == 0)
    def _():
        take(odd_in, even_in)

    @pl.when(parity == 1)
    def _():
        take(even_in, odd_in)

    run_copies(
        [
            pltpu.make_async_copy(held.at[place ^ hop], outs[hop], sems.at[hop])
            for hop in range(PLANE)
        ]
    )


def finish_kernel(head_size, roles, *refs):
    count = PLANE * len(CHUNKS)
    pieces = refs[:count]
    first_out, second_out, turned, sems = refs[count:]
    place = roles[0]
    per_device = HEADS // PLANE
    copies = []
    first = 0
    for chunk, heads in enumerate(CHUNKS):
        for hop in range(PLANE):
            group = place ^ hop
            row = pl.multiple_of((group * per_device + first) * head_size, 16)
            number = chunk * PLANE + hop
            copies.append(
                pltpu.make_async_copy(
                    pieces[number], turned.at[:, pl.ds(row, heads * head_size)], sems.at[number]
                )
            )
        first += heads
    run_copies(copies)
    first_out[...] = turned[0].T
    second_out[...] = turned[1].T


def body(queries, keys, values, cotangent, local_blocks, far_blocks, counts):
    tokens, width = queries.shape
    head_size = width // HEADS
    size = lax.axis_size("seq")
    planes = size // PLANE
    device = lax.axis_index("seq")
    level = device // PLANE
    roles = jnp.stack(
        [
            device % PLANE,
            level,
            level % 2,
            (level > 0).astype(jnp.int32),
            (level < planes - 1).astype(jnp.int32),
        ]
    ).astype(jnp.int32)

    def swap(array, hop):
        pairs = [(i, (i // PLANE) * PLANE + ((i % PLANE) ^ hop)) for i in range(size)]
        return lax.ppermute(array, "seq", pairs)

    def level_swap(array, odd):
        pairs = []
        for i in range(size):
            z = i // PLANE
            other = z + 1 if z % 2 == odd else z - 1
            pairs.append((i, i + (other - z) * PLANE if 0 <= other < planes else i ^ 1))
        return lax.ppermute(array, "seq", pairs)

    def piece(heads):
        return jax.ShapeDtypeStruct((2, heads * head_size, tokens), BF16)

    def prep(first, second, *lists):
        limits_shape = jax.ShapeDtypeStruct((PLANE * 2 * WINDOW * 2,), jnp.int32)
        return pl.pallas_call(
            lambda *refs: prep_kernel(head_size, len(lists), *refs),
            out_shape=[piece(heads) for heads in CHUNKS for _ in range(PLANE)]
            + ([limits_shape] if lists else []),
            in_specs=[SMEM, ANY, ANY] + [SMEM] * len(lists),
            out_specs=[ANY] * (PLANE * len(CHUNKS)) + ([SMEM] if lists else []),
            scratch_shapes=[
                pltpu.VMEM((2, tokens, width), BF16),
                pltpu.VMEM((2, width, tokens), BF16),
                pltpu.SemaphoreType.DMA((2,)),
                pltpu.SemaphoreType.DMA((PLANE * len(CHUNKS),)),
            ],
            compiler_params=params(),
            cost_estimate=cost(3),
        )(roles, first, second, *lists)

    def spread(parts):
        return [
            [parts[chunk * PLANE]]
            + [swap(parts[chunk * PLANE + hop], hop) for hop in range(1, PLANE)]
            for chunk in range(len(CHUNKS))
        ]

    key_held = spread(prep(keys, values))
    query_pieces = []
    key_pieces = []
    halos = []
    *query_ready, limits = prep(queries, cotangent, local_blocks, far_blocks, counts)
    query_held = spread(query_ready)
    for chunk, heads in enumerate(CHUNKS):
        held = key_held[chunk]
        held = after(held, query_ready)
        pair = jax.ShapeDtypeStruct((2, 2, heads * head_size, tokens), BF16)
        even, odd = pl.pallas_call(
            pack_kernel,
            out_shape=[pair, pair],
            in_specs=[SMEM] + [ANY] * PLANE,
            out_specs=[ANY, ANY],
            scratch_shapes=[
                pltpu.VMEM((PLANE, 2, heads * head_size, tokens), BF16),
                pltpu.SemaphoreType.DMA((PLANE,)),
            ],
            compiler_params=params(),
            cost_estimate=cost(2),
        )(roles, *held)
        halos.append((level_swap(even, 0), level_swap(odd, 1)))

    def main(chunk):
        heads = CHUNKS[chunk]
        even, odd = halos[chunk]
        shape = (heads, head_size, tokens)
        return pl.pallas_call(
            lambda *refs: main_kernel(head_size, heads, *refs),
            out_shape=[jax.ShapeDtypeStruct((2,) + shape, BF16)] * PLANE
            + [jax.ShapeDtypeStruct((PLANE, 2) + shape, BF16)]
            + [jax.ShapeDtypeStruct((2, 2) + shape, BF16)] * 2,
            in_specs=[SMEM, SMEM] + [ANY] * (2 * PLANE + 2),
            out_specs=[ANY] * (PLANE + 3),
            scratch_shapes=[
                pltpu.VMEM((CHAIN + 1, 2) + shape, BF16),
                pltpu.VMEM((PLANE, 2) + shape, BF16),
                pltpu.VMEM((PLANE, 2) + shape, BF16),
                pltpu.VMEM((CHAIN + 1, 2) + shape, F32),
                pltpu.VMEM((CHAIN + 1, 2) + shape, BF16),
                pltpu.VMEM((WINDOW * tokens, tokens), F32),
                pltpu.VMEM((WINDOW * tokens, tokens), F32),
                pltpu.VMEM((WINDOW * tokens, tokens), F32),
                pltpu.VMEM((WINDOW * tokens, tokens), F32),
                pltpu.VMEM((8, tokens), F32),
                pltpu.VMEM((8, tokens), F32),
                pltpu.VMEM((WINDOW * tokens, tokens), BF16),
                pltpu.VMEM((WINDOW * tokens, tokens), BF16),
                pltpu.SemaphoreType.DMA((2 * PLANE + 2,)),
            ],
            compiler_params=params(),
            cost_estimate=cost(6 * heads),
        )(
            roles,
            limits,
            *[part.reshape((2,) + shape) for part in key_held[chunk] + query_held[chunk]],
            even.reshape((2, 2) + shape),
            odd.reshape((2, 2) + shape),
        )

    def join(chunk, local, even, odd):
        heads = CHUNKS[chunk]
        flat = (2, heads * head_size, tokens)
        return pl.pallas_call(
            join_kernel,
            out_shape=[piece(heads)] * PLANE,
            in_specs=[SMEM] + [VMEM] * 3,
            out_specs=[ANY] * PLANE,
            scratch_shapes=[
                pltpu.VMEM((PLANE,) + flat, BF16),
                pltpu.SemaphoreType.DMA((PLANE,)),
            ],
            compiler_params=params(),
        )(roles, local.reshape((PLANE,) + flat), even.reshape((2,) + flat), odd.reshape((2,) + flat))

    def spread_one(parts):
        return [parts[0]] + [swap(parts[hop], hop) for hop in range(1, PLANE)]

    rounds = len(CHUNKS)
    results = [main(chunk) for chunk in range(rounds)]
    last = None
    returned = []
    for chunk in range(rounds):
        shape = (2, CHUNKS[chunk] * head_size, tokens)
        out = [part.reshape(shape) for part in results[chunk][:PLANE]]
        if chunk:
            out = after(out, last[1:] + list(returned[-1]))
        last = spread_one(out)
        query_pieces += last
        local, even, odd = results[chunk][PLANE:]
        returned.append((level_swap(even, 0), level_swap(odd, 1)))
    for chunk in range(rounds):
        local = results[chunk][PLANE]
        if chunk == rounds - 1:
            local = after([local], last[1:2] + [back[0]])[0]
        back = join(chunk, local, *returned[chunk])
        key_pieces += spread_one(back)

    def finish(parts):
        return pl.pallas_call(
            lambda *refs: finish_kernel(head_size, *refs),
            out_shape=[jax.ShapeDtypeStruct((tokens, width), BF16)] * 2,
            in_specs=[SMEM] + [ANY] * len(parts),
            out_specs=[VMEM, VMEM],
            scratch_shapes=[
                pltpu.VMEM((2, width, tokens), BF16),
                pltpu.SemaphoreType.DMA((len(parts),)),
            ],
            compiler_params=params(),
        )(roles, *parts)

    attended, query_grad = finish(query_pieces)
    key_grad, value_grad = finish(key_pieces)
    return attended, query_grad, key_grad, value_grad


def solution(mesh):
    rows = P(("groups", "seq"), None)
    return jax.shard_map(
        body,
        mesh=mesh,
        in_specs=(rows, rows, rows, rows, P("groups", None), P("groups", None), P("groups")),
        out_specs=(rows, rows, rows, rows),
        check_vma=False,
    )
```

```python
import math

import jax
import jax.numpy as jnp
from jax import lax
from jax.experimental import pallas as pl
from jax.experimental.pallas import tpu as pltpu
from jax.sharding import PartitionSpec as P

HEADS = 16
BLK = 128
PLANE = 4
CHUNKS = (2, 2)
FAR_UP = 2
WINDOW = 4
CHAIN = PLANE + FAR_UP + 1
STRIP = 64
F32 = jnp.float32
BF16 = jnp.bfloat16
HBM = pl.BlockSpec(memory_space=pltpu.HBM)
SMEM = pl.BlockSpec(memory_space=pltpu.SMEM)
VMEM = pl.BlockSpec(memory_space=pltpu.VMEM)


def params(mib=64):
    return pltpu.CompilerParams(vmem_limit_bytes=mib << 20)


def after(arrays, others):
    return list(lax.optimization_barrier((list(arrays), list(others)))[0])


def cost(microseconds):
    return pl.CostEstimate(
        flops=microseconds * 1_000_000_000, bytes_accessed=1_000_000, transcendentals=0
    )


def place_of():
    return lax.axis_index("seq") % PLANE


def level_of():
    return lax.axis_index("seq") // PLANE


def run_copies(copies):
    for copy in copies:
        copy.start()
    for copy in copies:
        copy.wait()


def prep_kernel(head_size, chunks, lists, first_in, second_in, *refs):
    lists_in, refs = refs[:lists], refs[lists:]
    count = PLANE * len(chunks)
    outs = refs[:count]
    rows, turned, in_sems, sems = refs[-4:]
    width = rows.shape[2]
    begin = PLANE * sum(CHUNKS[: chunks[0]]) * head_size
    loads = [
        pltpu.make_async_copy(ref.at[:, pl.ds(begin, width)], rows.at[index], in_sems.at[index])
        for index, ref in enumerate((first_in, second_in))
    ]
    for load in loads:
        load.start()
    if lists:
        find_limits(*lists_in, refs[count])
    for index, load in enumerate(loads):
        load.wait()
        turned[index] = rows[index].T
    place = place_of()
    copies = []
    first = 0
    for number, chunk in enumerate(chunks):
        span = CHUNKS[chunk] * head_size
        for hop in range(PLANE):
            row = pl.multiple_of(first + (place ^ hop) * span, 16)
            slot = number * PLANE + hop
            copies.append(
                pltpu.make_async_copy(
                    turned.at[:, pl.ds(row, span)], outs[slot], sems.at[slot]
                )
            )
        first += PLANE * span
    run_copies(copies)


def find_limits(local_blocks, far_blocks, counts, out):
    blocks = counts.shape[0]
    first = level_of() * (PLANE * 2)
    for query in range(PLANE * 2):
        listed = [local_blocks[first + query, s] for s in range(local_blocks.shape[1])]
        listed += [far_blocks[first + query, s] for s in range(far_blocks.shape[1])]
        for slot in range(WINDOW * 2):
            key = first - 2 * FAR_UP + (query // 2) * 2 + slot
            found = listed[0] == key
            for entry in listed[1:]:
                found = found | (entry == key)
            inside = (key >= 0) & (key < blocks)
            count = counts[jnp.clip(key, 0, blocks - 1)]
            out[query * WINDOW * 2 + slot] = jnp.where(found & inside, count, 0)


def pack_kernel(*refs):
    pieces = refs[:PLANE]
    even, odd = refs[PLANE : PLANE + 2]
    plane, sems = refs[PLANE + 2 :]
    place, parity = place_of(), level_of() % 2
    run_copies(
        [
            pltpu.make_async_copy(pieces[hop], plane.at[place ^ hop], sems.at[hop])
            for hop in range(PLANE)
        ]
    )
    run_copies(
        [
            pltpu.make_async_copy(plane.at[pl.ds(2 - 2 * parity, 2)], even, sems.at[0]),
            pltpu.make_async_copy(plane.at[pl.ds(2 * parity, 2)], odd, sems.at[1]),
        ]
    )


def dot(a, b, left, right):
    return lax.dot_general(a, b, (((left,), (right,)), ((), ())), preferred_element_type=F32)


def main_kernel(head_size, heads, limits, *refs):
    key_pieces = refs[:PLANE]
    query_pieces = refs[PLANE : 2 * PLANE]
    even_in, odd_in = refs[2 * PLANE : 2 * PLANE + 2]
    rest = refs[2 * PLANE + 2 :]
    outs = rest[:PLANE]
    local_out, even_out, odd_out = rest[PLANE : PLANE + 3]
    chain, query, result, key_sums, sums = rest[PLANE + 3 : PLANE + 8]
    scores, grads, peaks = (rest[PLANE + 8 + 2 * i : PLANE + 10 + 2 * i] for i in range(3))
    weights, grad_scores, sems = rest[PLANE + 14 :]
    place, parity = place_of(), level_of() % 2
    copies = []
    for hop in range(PLANE):
        unit = place ^ hop
        copies.append(
            pltpu.make_async_copy(key_pieces[hop], chain.at[FAR_UP + unit], sems.at[2 * hop])
        )
        copies.append(
            pltpu.make_async_copy(query_pieces[hop], query.at[unit], sems.at[2 * hop + 1])
        )
    above = FAR_UP + PLANE
    copies.append(
        pltpu.make_async_copy(
            even_in, chain.at[pl.ds((1 - parity) * above, 2)], sems.at[2 * PLANE]
        )
    )
    copies.append(
        pltpu.make_async_copy(odd_in, chain.at[pl.ds(parity * above, 2)], sems.at[2 * PLANE + 1])
    )
    for copy in copies:
        copy.start()
    key_sums[...] = jnp.zeros_like(key_sums)
    for copy in copies:
        copy.wait()

    scale = 1.0 / math.sqrt(head_size)
    rate = scale * math.log2(math.e)
    tokens = 2 * BLK
    row = lax.broadcasted_iota(jnp.int32, (BLK, tokens), 0)
    lane = lax.broadcasted_iota(jnp.int32, (1, tokens), 1)
    steps = heads * PLANE

    def score(index, slot, k, peak):
        head, unit = index // PLANE, index % PLANE
        tile = dot(chain[unit + k, 0, head], query[unit, 0, head], 0, 0)
        for half in range(2):
            block = 2 * k + half
            base = unit * 2 * WINDOW * 2 + block
            limit = jnp.where(lane < BLK, limits[base], limits[base + WINDOW * 2])
            for at in range(0, BLK, STRIP):
                part = tile[half * BLK + at : half * BLK + at + STRIP]
                part = jnp.where(row[at : at + STRIP] < limit, part, -1e30)
                top = jnp.max(part.reshape(STRIP // 8, 8, tokens), axis=0)
                peak = top if peak is None else jnp.maximum(peak, top)
                scores[slot][block * BLK + at : block * BLK + at + STRIP] = part
        return peak

    def keep_peak(slot, peak):
        peak = jnp.max(peak, axis=0, keepdims=True)
        peaks[slot][...] = jnp.broadcast_to(peak, (8, tokens))

    def grad(index, slot, k):
        head, unit = index // PLANE, index % PLANE
        grads[slot][k * tokens : (k + 1) * tokens] = dot(
            chain[unit + k, 1, head], query[unit, 1, head], 0, 0
        )

    def step(index, now, later, final=False):
        head, unit = index // PLANE, index % PLANE
        query_t = query[unit, 0, head]
        grad_wide = query[unit, 1, head].astype(F32)
        peak = peaks[now][0:1]
        total = out_t = later_peak = query_grad = None
        for k in range(WINDOW):
            span = slice(k * tokens, (k + 1) * tokens)
            if not final:
                later_peak = score(index + 1, later, k, later_peak)
            for at in range(k * tokens, (k + 1) * tokens, STRIP):
                power = jnp.exp2((scores[now][at : at + STRIP] - peak) * rate)
                part = jnp.sum(power.reshape(STRIP // 8, 8, tokens), axis=0)
                total = part if total is None else total + part
                weights[at : at + STRIP] = power.astype(BF16)
            part = dot(chain[unit + k, 1, head], weights[span], 1, 0)
            out_t = part if k == 0 else out_t + part
        if not final:
            keep_peak(later, later_peak)
        inverse = 1.0 / jnp.sum(total, axis=0, keepdims=True)
        attended = (out_t * inverse).astype(BF16)
        delta = jnp.sum(grad_wide * attended.astype(F32), axis=0, keepdims=True)
        grad_scaled = (grad_wide * inverse).astype(BF16)
        query_scaled = (query_t.astype(F32) * inverse).astype(BF16)
        for k in range(WINDOW):
            span = slice(k * tokens, (k + 1) * tokens)
            key_sums[unit + k, 1, head] += dot(grad_scaled, weights[span], 1, 1)
        for k in range(WINDOW):
            span = slice(k * tokens, (k + 1) * tokens)
            if not final:
                grad(index + 1, later, k)
            for at in range(k * tokens, (k + 1) * tokens, STRIP):
                change = (grads[now][at : at + STRIP] - delta).astype(BF16)
                grad_scores[at : at + STRIP] = weights[at : at + STRIP] * change
            part = dot(chain[unit + k, 0, head], grad_scores[span], 1, 0)
            query_grad = part if k == 0 else query_grad + part
            key_sums[unit + k, 0, head] += dot(query_scaled, grad_scores[span], 1, 1)
        result[unit, 0, head] = attended
        result[unit, 1, head] = (query_grad * (inverse * scale)).astype(BF16)

    first_peak = None
    for k in range(WINDOW):
        first_peak = score(0, 0, k, first_peak)
        grad(0, 0, k)
    keep_peak(0, first_peak)

    def two_steps(index, carry):
        step(2 * index, 0, 1)
        step(2 * index + 1, 1, 0)
        return carry

    lax.fori_loop(0, steps // 2 - 1, two_steps, 0)
    step(steps - 2, 0, 1)
    step(steps - 1, 1, 0, final=True)
    copies = [
        pltpu.make_async_copy(result.at[place ^ hop], outs[hop], sems.at[hop])
        for hop in range(PLANE)
    ]
    for copy in copies:
        copy.start()
    for unit in range(CHAIN + 1):
        sums[unit, 0] = (key_sums[unit, 0] * scale).astype(BF16)
        sums[unit, 1] = key_sums[unit, 1].astype(BF16)
    more = [
        pltpu.make_async_copy(sums.at[pl.ds(FAR_UP, PLANE)], local_out, sems.at[PLANE]),
        pltpu.make_async_copy(
            sums.at[pl.ds((1 - parity) * above, 2)], even_out, sems.at[PLANE + 1]
        ),
        pltpu.make_async_copy(sums.at[pl.ds(parity * above, 2)], odd_out, sems.at[PLANE + 2]),
    ]
    for copy in more:
        copy.start()
    for copy in copies + more:
        copy.wait()


def join_kernel(planes, local, even_in, odd_in, *refs):
    outs = refs[:PLANE]
    held, sems = refs[PLANE:]
    place, parity = place_of(), level_of() % 2
    level = level_of()
    held[...] = local[...]

    def take(below, above):
        @pl.when(level > 0)
        def _():
            held[0] = (held[0].astype(F32) + below[0].astype(F32)).astype(BF16)

        @pl.when(level < planes - 1)
        def _():
            for unit in range(2):
                held[2 + unit] = (held[2 + unit].astype(F32) + above[unit].astype(F32)).astype(
                    BF16
                )

    @pl.when(parity == 0)
    def _():
        take(odd_in, even_in)

    @pl.when(parity == 1)
    def _():
        take(even_in, odd_in)

    run_copies(
        [
            pltpu.make_async_copy(held.at[place ^ hop], outs[hop], sems.at[hop])
            for hop in range(PLANE)
        ]
    )


def finish_kernel(head_size, chunks, held, *refs):
    count = PLANE * len(chunks)
    pieces = refs[:count]
    outs = refs[count + held : count + held + 2]
    turned, rows, sems, out_sems = refs[count + held + 2 :]
    place = place_of()
    begin = PLANE * sum(CHUNKS[: chunks[0]]) * head_size
    width = rows.shape[2]
    loads = []
    first = 0
    for number, chunk in enumerate(chunks):
        span = CHUNKS[chunk] * head_size
        for hop in range(PLANE):
            row = pl.multiple_of(first + (place ^ hop) * span, 16)
            for tensor in range(2):
                loads.append(
                    pltpu.make_async_copy(
                        pieces[number * PLANE + hop].at[tensor],
                        turned.at[tensor, pl.ds(row, span)],
                        sems.at[tensor, number * PLANE + hop],
                    )
                )
        first += PLANE * span
    for load in loads:
        load.start()
    stores = []
    for tensor in range(2):
        for load in loads[tensor::2]:
            load.wait()
        rows[tensor] = turned[tensor].T
        store = pltpu.make_async_copy(
            rows.at[tensor], outs[tensor].at[:, pl.ds(begin, width)], out_sems.at[tensor]
        )
        store.start()
        stores.append(store)
    for store in stores:
        store.wait()


def body(queries, keys, values, cotangent, local_blocks, far_blocks, counts):
    tokens, width = queries.shape
    head_size = width // HEADS
    size = lax.axis_size("seq")
    planes = size // PLANE
    def swap(array, hop):
        pairs = [(i, (i // PLANE) * PLANE + ((i % PLANE) ^ hop)) for i in range(size)]
        return lax.ppermute(array, "seq", pairs)

    def level_swap(array, odd):
        pairs = []
        for i in range(size):
            z = i // PLANE
            other = z + 1 if z % 2 == odd else z - 1
            pairs.append((i, i + (other - z) * PLANE if 0 <= other < planes else i ^ 1))
        return lax.ppermute(array, "seq", pairs)

    def piece(heads):
        return jax.ShapeDtypeStruct((2, heads * head_size, tokens), BF16)

    def prep(first, second, chunks, *lists):
        span = PLANE * sum(CHUNKS[chunk] for chunk in chunks) * head_size
        limits_shape = jax.ShapeDtypeStruct((PLANE * 2 * WINDOW * 2,), jnp.int32)
        count = PLANE * len(chunks)
        return pl.pallas_call(
            lambda *refs: prep_kernel(head_size, chunks, len(lists), *refs),
            out_shape=[piece(CHUNKS[chunk]) for chunk in chunks for _ in range(PLANE)]
            + ([limits_shape] if lists else []),
            in_specs=[HBM, HBM] + [SMEM] * len(lists),
            out_specs=[HBM] * count + ([SMEM] if lists else []),
            scratch_shapes=[
                pltpu.VMEM((2, tokens, span), BF16),
                pltpu.VMEM((2, span, tokens), BF16),
                pltpu.SemaphoreType.DMA((2,)),
                pltpu.SemaphoreType.DMA((count,)),
            ],
            compiler_params=params(),
            cost_estimate=cost(3),
        )(first, second, *lists)

    def spread(parts):
        return [parts[0]] + [swap(parts[hop], hop) for hop in range(1, PLANE)]

    rounds = len(CHUNKS)
    every = tuple(range(rounds))
    key_held = [
        spread(key_ready[PLANE * chunk : PLANE * (chunk + 1)])
        for key_ready in [prep(keys, values, every)]
        for chunk in every
    ]
    query_pieces = []
    key_pieces = []
    halos = []
    *query_ready, limits = prep(queries, cotangent, every, local_blocks, far_blocks, counts)
    query_held = [spread(query_ready[PLANE * chunk : PLANE * (chunk + 1)]) for chunk in every]
    for chunk, heads in enumerate(CHUNKS):
        held = key_held[chunk]
        held = after(held, query_ready)
        pair = jax.ShapeDtypeStruct((2, 2, heads * head_size, tokens), BF16)
        even, odd = pl.pallas_call(
            pack_kernel,
            out_shape=[pair, pair],
            in_specs=[HBM] * PLANE,
            out_specs=[HBM, HBM],
            scratch_shapes=[
                pltpu.VMEM((PLANE, 2, heads * head_size, tokens), BF16),
                pltpu.SemaphoreType.DMA((PLANE,)),
            ],
            compiler_params=params(),
            cost_estimate=cost(2),
        )(*held)
        halos.append((level_swap(even, 0), level_swap(odd, 1)))

    def main(chunk):
        heads = CHUNKS[chunk]
        even, odd = halos[chunk]
        shape = (heads, head_size, tokens)
        return pl.pallas_call(
            lambda *refs: main_kernel(head_size, heads, *refs),
            out_shape=[jax.ShapeDtypeStruct((2,) + shape, BF16)] * PLANE
            + [jax.ShapeDtypeStruct((PLANE, 2) + shape, BF16)]
            + [jax.ShapeDtypeStruct((2, 2) + shape, BF16)] * 2,
            in_specs=[SMEM] + [HBM] * (2 * PLANE + 2),
            out_specs=[HBM] * (PLANE + 3),
            scratch_shapes=[
                pltpu.VMEM((CHAIN + 1, 2) + shape, BF16),
                pltpu.VMEM((PLANE, 2) + shape, BF16),
                pltpu.VMEM((PLANE, 2) + shape, BF16),
                pltpu.VMEM((CHAIN + 1, 2) + shape, F32),
                pltpu.VMEM((CHAIN + 1, 2) + shape, BF16),
                pltpu.VMEM((WINDOW * tokens, tokens), F32),
                pltpu.VMEM((WINDOW * tokens, tokens), F32),
                pltpu.VMEM((WINDOW * tokens, tokens), F32),
                pltpu.VMEM((WINDOW * tokens, tokens), F32),
                pltpu.VMEM((8, tokens), F32),
                pltpu.VMEM((8, tokens), F32),
                pltpu.VMEM((WINDOW * tokens, tokens), BF16),
                pltpu.VMEM((WINDOW * tokens, tokens), BF16),
                pltpu.SemaphoreType.DMA((2 * PLANE + 2,)),
            ],
            compiler_params=params(),
            cost_estimate=cost(6 * heads),
        )(
            limits,
            *[part.reshape((2,) + shape) for part in key_held[chunk] + query_held[chunk]],
            even.reshape((2, 2) + shape),
            odd.reshape((2, 2) + shape),
        )

    def join(chunk, local, even, odd):
        heads = CHUNKS[chunk]
        flat = (2, heads * head_size, tokens)
        return pl.pallas_call(
            lambda *refs: join_kernel(size // PLANE, *refs),
            out_shape=[piece(heads)] * PLANE,
            in_specs=[VMEM] * 3,
            out_specs=[HBM] * PLANE,
            scratch_shapes=[
                pltpu.VMEM((PLANE,) + flat, BF16),
                pltpu.SemaphoreType.DMA((PLANE,)),
            ],
            compiler_params=params(),
        )(local.reshape((PLANE,) + flat), even.reshape((2,) + flat), odd.reshape((2,) + flat))

    results = [main(chunk) for chunk in range(rounds)]
    last = None
    returned = []
    for chunk in range(rounds):
        shape = (2, CHUNKS[chunk] * head_size, tokens)
        out = [part.reshape(shape) for part in results[chunk][:PLANE]]
        if chunk:
            out = after(out, last[1:] + list(returned[-1]))
        last = spread(out)
        query_pieces += last
        local, even, odd = results[chunk][PLANE:]
        returned.append((level_swap(even, 0), level_swap(odd, 1)))
    for chunk in range(rounds):
        local = results[chunk][PLANE]
        if chunk == rounds - 1:
            local = after([local], last[1:2] + [back[0]])[0]
        back = join(chunk, local, *returned[chunk])
        key_pieces += spread(back)

    def finish(parts, chunks, held=()):
        span = PLANE * sum(CHUNKS[chunk] for chunk in chunks) * head_size
        return pl.pallas_call(
            lambda *refs: finish_kernel(head_size, chunks, len(held), *refs),
            out_shape=[jax.ShapeDtypeStruct((tokens, width), BF16)] * 2,
            in_specs=[HBM] * (len(parts) + len(held)),
            out_specs=[HBM, HBM],
            scratch_shapes=[
                pltpu.VMEM((2, span, tokens), BF16),
                pltpu.VMEM((2, tokens, span), BF16),
                pltpu.SemaphoreType.DMA((2, len(parts))),
                pltpu.SemaphoreType.DMA((2,)),
            ],
            input_output_aliases={len(parts) + index: index for index in range(len(held))},
            compiler_params=params(),
            cost_estimate=cost(3),
        )(*parts, *held)

    attended, query_grad = finish(query_pieces, every)
    sums = ()
    for chunk in every:
        sums = finish(key_pieces[PLANE * chunk : PLANE * (chunk + 1)], (chunk,), sums)
    return attended, query_grad, *sums


def solution(mesh):
    rows = P(("groups", "seq"), None)
    return jax.shard_map(
        body,
        mesh=mesh,
        in_specs=(rows, rows, rows, rows, P("groups", None), P("groups", None), P("groups")),
        out_specs=(rows, rows, rows, rows),
        check_vma=False,
    )
```

```python
import math

import jax
import jax.numpy as jnp
from jax import lax
from jax.experimental import pallas as pl
from jax.experimental.pallas import tpu as pltpu
from jax.sharding import PartitionSpec as P

HEADS = 16
BLK = 128
PLANE = 4
CHUNKS = (2, 2)
FAR_UP = 2
WINDOW = 4
CHAIN = PLANE + FAR_UP + 1
STRIP = 64
F32 = jnp.float32
BF16 = jnp.bfloat16
HBM = pl.BlockSpec(memory_space=pltpu.HBM)
SMEM = pl.BlockSpec(memory_space=pltpu.SMEM)
VMEM = pl.BlockSpec(memory_space=pltpu.VMEM)


def params(mib=64):
    return pltpu.CompilerParams(vmem_limit_bytes=mib << 20)


def after(arrays, others):
    if not others:
        return list(arrays)
    return list(lax.optimization_barrier((list(arrays), list(others)))[0])


def cost(microseconds):
    return pl.CostEstimate(
        flops=int(microseconds * 1_000_000_000), bytes_accessed=1_000_000, transcendentals=0
    )


def place_of():
    return lax.axis_index("seq") % PLANE


def level_of():
    return lax.axis_index("seq") // PLANE


def run_copies(copies):
    for copy in copies:
        copy.start()
    for copy in copies:
        copy.wait()


def prep_kernel(head_size, chunks, lists, first_in, second_in, *refs):
    lists_in, refs = refs[:lists], refs[lists:]
    count = PLANE * len(chunks)
    outs = refs[:count]
    rows, turned, in_sems, sems = refs[-4:]
    width = rows.shape[2]
    begin = PLANE * sum(CHUNKS[: chunks[0]]) * head_size
    loads = [
        pltpu.make_async_copy(ref.at[:, pl.ds(begin, width)], rows.at[index], in_sems.at[index])
        for index, ref in enumerate((first_in, second_in))
    ]
    for load in loads:
        load.start()
    if lists:
        find_limits(*lists_in, refs[count])
    for index, load in enumerate(loads):
        load.wait()
        turned[index] = rows[index].T
    place = place_of()
    copies = []
    first = 0
    for number, chunk in enumerate(chunks):
        span = CHUNKS[chunk] * head_size
        for hop in range(PLANE):
            row = pl.multiple_of(first + (place ^ hop) * span, 16)
            slot = number * PLANE + hop
            copies.append(
                pltpu.make_async_copy(
                    turned.at[:, pl.ds(row, span)], outs[slot], sems.at[slot]
                )
            )
        first += PLANE * span
    run_copies(copies)


def find_limits(local_blocks, far_blocks, counts, out):
    blocks = counts.shape[0]
    first = level_of() * (PLANE * 2)
    for query in range(PLANE * 2):
        listed = [local_blocks[first + query, s] for s in range(local_blocks.shape[1])]
        listed += [far_blocks[first + query, s] for s in range(far_blocks.shape[1])]
        for slot in range(WINDOW * 2):
            key = first - 2 * FAR_UP + (query // 2) * 2 + slot
            found = listed[0] == key
            for entry in listed[1:]:
                found = found | (entry == key)
            inside = (key >= 0) & (key < blocks)
            count = counts[jnp.clip(key, 0, blocks - 1)]
            out[query * WINDOW * 2 + slot] = jnp.where(found & inside, count, 0)


def pack_kernel(*refs):
    pieces = refs[:PLANE]
    even, odd = refs[PLANE : PLANE + 2]
    plane, sems = refs[PLANE + 2 :]
    place, parity = place_of(), level_of() % 2
    run_copies(
        [
            pltpu.make_async_copy(pieces[hop], plane.at[place ^ hop], sems.at[hop])
            for hop in range(PLANE)
        ]
    )
    run_copies(
        [
            pltpu.make_async_copy(plane.at[pl.ds(2 - 2 * parity, 2)], even, sems.at[0]),
            pltpu.make_async_copy(plane.at[pl.ds(2 * parity, 2)], odd, sems.at[1]),
        ]
    )


def dot(a, b, left, right):
    return lax.dot_general(a, b, (((left,), (right,)), ((), ())), preferred_element_type=F32)


def main_kernel(head_size, heads, limits, *refs):
    key_pieces = refs[:PLANE]
    query_pieces = refs[PLANE : 2 * PLANE]
    even_in, odd_in = refs[2 * PLANE : 2 * PLANE + 2]
    rest = refs[2 * PLANE + 2 :]
    outs = rest[:PLANE]
    local_out, even_out, odd_out = rest[PLANE : PLANE + 3]
    chain, query, result, key_sums, sums = rest[PLANE + 3 : PLANE + 8]
    scores, grads, peaks = (rest[PLANE + 8 + 2 * i : PLANE + 10 + 2 * i] for i in range(3))
    weights, grad_scores, sems = rest[PLANE + 14 :]
    place, parity = place_of(), level_of() % 2
    copies = []
    for hop in range(PLANE):
        unit = place ^ hop
        copies.append(
            pltpu.make_async_copy(key_pieces[hop], chain.at[FAR_UP + unit], sems.at[2 * hop])
        )
        copies.append(
            pltpu.make_async_copy(query_pieces[hop], query.at[unit], sems.at[2 * hop + 1])
        )
    above = FAR_UP + PLANE
    copies.append(
        pltpu.make_async_copy(
            even_in, chain.at[pl.ds((1 - parity) * above, 2)], sems.at[2 * PLANE]
        )
    )
    copies.append(
        pltpu.make_async_copy(odd_in, chain.at[pl.ds(parity * above, 2)], sems.at[2 * PLANE + 1])
    )
    for copy in copies:
        copy.start()
    key_sums[...] = jnp.zeros_like(key_sums)
    for copy in copies:
        copy.wait()

    scale = 1.0 / math.sqrt(head_size)
    rate = scale * math.log2(math.e)
    tokens = 2 * BLK
    row = lax.broadcasted_iota(jnp.int32, (BLK, tokens), 0)
    lane = lax.broadcasted_iota(jnp.int32, (1, tokens), 1)
    steps = heads * PLANE

    def score(index, slot, k, peak):
        head, unit = index // PLANE, index % PLANE
        tile = dot(chain[unit + k, 0, head], query[unit, 0, head], 0, 0)
        for half in range(2):
            block = 2 * k + half
            base = unit * 2 * WINDOW * 2 + block
            limit = jnp.where(lane < BLK, limits[base], limits[base + WINDOW * 2])
            for at in range(0, BLK, STRIP):
                part = tile[half * BLK + at : half * BLK + at + STRIP]
                part = jnp.where(row[at : at + STRIP] < limit, part, -1e30)
                top = jnp.max(part.reshape(STRIP // 8, 8, tokens), axis=0)
                peak = top if peak is None else jnp.maximum(peak, top)
                scores[slot][block * BLK + at : block * BLK + at + STRIP] = part
        return peak

    def keep_peak(slot, peak):
        peak = jnp.max(peak, axis=0, keepdims=True)
        peaks[slot][...] = jnp.broadcast_to(peak, (8, tokens))

    def grad(index, slot, k):
        head, unit = index // PLANE, index % PLANE
        grads[slot][k * tokens : (k + 1) * tokens] = dot(
            chain[unit + k, 1, head], query[unit, 1, head], 0, 0
        )

    def step(index, now, later, final=False):
        head, unit = index // PLANE, index % PLANE
        query_t = query[unit, 0, head]
        grad_wide = query[unit, 1, head].astype(F32)
        peak = peaks[now][0:1]
        total = out_t = later_peak = query_grad = None
        for k in range(WINDOW):
            span = slice(k * tokens, (k + 1) * tokens)
            if not final:
                later_peak = score(index + 1, later, k, later_peak)
            for at in range(k * tokens, (k + 1) * tokens, STRIP):
                power = jnp.exp2((scores[now][at : at + STRIP] - peak) * rate)
                part = jnp.sum(power.reshape(STRIP // 8, 8, tokens), axis=0)
                total = part if total is None else total + part
                weights[at : at + STRIP] = power.astype(BF16)
            part = dot(chain[unit + k, 1, head], weights[span], 1, 0)
            out_t = part if k == 0 else out_t + part
        if not final:
            keep_peak(later, later_peak)
        inverse = 1.0 / jnp.sum(total, axis=0, keepdims=True)
        attended = (out_t * inverse).astype(BF16)
        delta = jnp.sum(grad_wide * attended.astype(F32), axis=0, keepdims=True)
        grad_scaled = (grad_wide * inverse).astype(BF16)
        query_scaled = (query_t.astype(F32) * inverse).astype(BF16)
        for k in range(WINDOW):
            span = slice(k * tokens, (k + 1) * tokens)
            key_sums[unit + k, 1, head] += dot(grad_scaled, weights[span], 1, 1)
        for k in range(WINDOW):
            span = slice(k * tokens, (k + 1) * tokens)
            if not final:
                grad(index + 1, later, k)
            for at in range(k * tokens, (k + 1) * tokens, STRIP):
                change = (grads[now][at : at + STRIP] - delta).astype(BF16)
                grad_scores[at : at + STRIP] = weights[at : at + STRIP] * change
            part = dot(chain[unit + k, 0, head], grad_scores[span], 1, 0)
            query_grad = part if k == 0 else query_grad + part
            key_sums[unit + k, 0, head] += dot(query_scaled, grad_scores[span], 1, 1)
        result[unit, 0, head] = attended
        result[unit, 1, head] = (query_grad * (inverse * scale)).astype(BF16)

    first_peak = None
    for k in range(WINDOW):
        first_peak = score(0, 0, k, first_peak)
        grad(0, 0, k)
    keep_peak(0, first_peak)

    def two_steps(index, carry):
        step(2 * index, 0, 1)
        step(2 * index + 1, 1, 0)
        return carry

    lax.fori_loop(0, steps // 2 - 1, two_steps, 0)
    step(steps - 2, 0, 1)
    step(steps - 1, 1, 0, final=True)
    copies = [
        pltpu.make_async_copy(result.at[place ^ hop], outs[hop], sems.at[hop])
        for hop in range(PLANE)
    ]
    for copy in copies:
        copy.start()
    for unit in range(CHAIN + 1):
        sums[unit, 0] = (key_sums[unit, 0] * scale).astype(BF16)
        sums[unit, 1] = key_sums[unit, 1].astype(BF16)
    more = [
        pltpu.make_async_copy(sums.at[pl.ds(FAR_UP, PLANE)], local_out, sems.at[PLANE]),
        pltpu.make_async_copy(
            sums.at[pl.ds((1 - parity) * above, 2)], even_out, sems.at[PLANE + 1]
        ),
        pltpu.make_async_copy(sums.at[pl.ds(parity * above, 2)], odd_out, sems.at[PLANE + 2]),
    ]
    for copy in more:
        copy.start()
    for copy in copies + more:
        copy.wait()


def join_kernel(planes, local, even_in, odd_in, *refs):
    outs = refs[:PLANE]
    held, sems = refs[PLANE:]
    place, parity = place_of(), level_of() % 2
    level = level_of()
    held[...] = local[...]

    def take(below, above):
        @pl.when(level > 0)
        def _():
            held[0] = (held[0].astype(F32) + below[0].astype(F32)).astype(BF16)

        @pl.when(level < planes - 1)
        def _():
            for unit in range(2):
                held[2 + unit] = (held[2 + unit].astype(F32) + above[unit].astype(F32)).astype(
                    BF16
                )

    @pl.when(parity == 0)
    def _():
        take(odd_in, even_in)

    @pl.when(parity == 1)
    def _():
        take(even_in, odd_in)

    run_copies(
        [
            pltpu.make_async_copy(held.at[place ^ hop], outs[hop], sems.at[hop])
            for hop in range(PLANE)
        ]
    )


def finish_kernel(head_size, chunks, held, *refs):
    count = PLANE * len(chunks)
    pieces = refs[:count]
    outs = refs[count + held : count + held + 2]
    turned, rows, sems, out_sems = refs[count + held + 2 :]
    place = place_of()
    begin = PLANE * sum(CHUNKS[: chunks[0]]) * head_size
    width = rows.shape[2]
    loads = []
    first = 0
    for number, chunk in enumerate(chunks):
        span = CHUNKS[chunk] * head_size
        for hop in range(PLANE):
            row = pl.multiple_of(first + (place ^ hop) * span, 16)
            for tensor in range(2):
                loads.append(
                    pltpu.make_async_copy(
                        pieces[number * PLANE + hop].at[tensor],
                        turned.at[tensor, pl.ds(row, span)],
                        sems.at[tensor, number * PLANE + hop],
                    )
                )
        first += PLANE * span
    for load in loads:
        load.start()
    stores = []
    for tensor in range(2):
        for load in loads[tensor::2]:
            load.wait()
        rows[tensor] = turned[tensor].T
        store = pltpu.make_async_copy(
            rows.at[tensor], outs[tensor].at[:, pl.ds(begin, width)], out_sems.at[tensor]
        )
        store.start()
        stores.append(store)
    for store in stores:
        store.wait()


def body(queries, keys, values, cotangent, local_blocks, far_blocks, counts):
    tokens, width = queries.shape
    head_size = width // HEADS
    size = lax.axis_size("seq")
    planes = size // PLANE
    def swap(array, hop):
        pairs = [(i, (i // PLANE) * PLANE + ((i % PLANE) ^ hop)) for i in range(size)]
        return lax.ppermute(array, "seq", pairs)

    def level_swap(array, odd):
        pairs = []
        for i in range(size):
            z = i // PLANE
            other = z + 1 if z % 2 == odd else z - 1
            pairs.append((i, i + (other - z) * PLANE if 0 <= other < planes else i ^ 1))
        return lax.ppermute(array, "seq", pairs)

    def piece(heads):
        return jax.ShapeDtypeStruct((2, heads * head_size, tokens), BF16)

    def prep(first, second, chunks, *lists):
        span = PLANE * sum(CHUNKS[chunk] for chunk in chunks) * head_size
        limits_shape = jax.ShapeDtypeStruct((PLANE * 2 * WINDOW * 2,), jnp.int32)
        count = PLANE * len(chunks)
        return pl.pallas_call(
            lambda *refs: prep_kernel(head_size, chunks, len(lists), *refs),
            out_shape=[piece(CHUNKS[chunk]) for chunk in chunks for _ in range(PLANE)]
            + ([limits_shape] if lists else []),
            in_specs=[HBM, HBM] + [SMEM] * len(lists),
            out_specs=[HBM] * count + ([SMEM] if lists else []),
            scratch_shapes=[
                pltpu.VMEM((2, tokens, span), BF16),
                pltpu.VMEM((2, span, tokens), BF16),
                pltpu.SemaphoreType.DMA((2,)),
                pltpu.SemaphoreType.DMA((count,)),
            ],
            compiler_params=params(),
            cost_estimate=cost(3),
        )(first, second, *lists)

    def spread(parts):
        moved = {hop: swap(parts[hop], hop) for hop in (1, 2, 3)}
        return [parts[0]] + [moved[hop] for hop in range(1, PLANE)]

    rounds = len(CHUNKS)
    every = tuple(range(rounds))
    key_held = [
        spread(key_ready[PLANE * chunk : PLANE * (chunk + 1)])
        for key_ready in [prep(keys, values, every)]
        for chunk in every
    ]
    query_pieces = []
    key_pieces = []
    halos = []
    *query_ready, limits = prep(queries, cotangent, every, local_blocks, far_blocks, counts)
    query_held = [spread(query_ready[PLANE * chunk : PLANE * (chunk + 1)]) for chunk in every]
    for chunk, heads in enumerate(CHUNKS):
        held = key_held[chunk]
        held = after(held, query_ready if chunk else query_ready)
        pair = jax.ShapeDtypeStruct((2, 2, heads * head_size, tokens), BF16)
        even, odd = pl.pallas_call(
            pack_kernel,
            out_shape=[pair, pair],
            in_specs=[HBM] * PLANE,
            out_specs=[HBM, HBM],
            scratch_shapes=[
                pltpu.VMEM((PLANE, 2, heads * head_size, tokens), BF16),
                pltpu.SemaphoreType.DMA((PLANE,)),
            ],
            compiler_params=params(),
            cost_estimate=cost(2),
        )(*held)
        halos.append((level_swap(even, 0), level_swap(odd, 1)))

    def main(chunk):
        heads = CHUNKS[chunk]
        even, odd = halos[chunk]
        shape = (heads, head_size, tokens)
        return pl.pallas_call(
            lambda *refs: main_kernel(head_size, heads, *refs),
            out_shape=[jax.ShapeDtypeStruct((2,) + shape, BF16)] * PLANE
            + [jax.ShapeDtypeStruct((PLANE, 2) + shape, BF16)]
            + [jax.ShapeDtypeStruct((2, 2) + shape, BF16)] * 2,
            in_specs=[SMEM] + [HBM] * (2 * PLANE + 2),
            out_specs=[HBM] * (PLANE + 3),
            scratch_shapes=[
                pltpu.VMEM((CHAIN + 1, 2) + shape, BF16),
                pltpu.VMEM((PLANE, 2) + shape, BF16),
                pltpu.VMEM((PLANE, 2) + shape, BF16),
                pltpu.VMEM((CHAIN + 1, 2) + shape, F32),
                pltpu.VMEM((CHAIN + 1, 2) + shape, BF16),
                pltpu.VMEM((WINDOW * tokens, tokens), F32),
                pltpu.VMEM((WINDOW * tokens, tokens), F32),
                pltpu.VMEM((WINDOW * tokens, tokens), F32),
                pltpu.VMEM((WINDOW * tokens, tokens), F32),
                pltpu.VMEM((8, tokens), F32),
                pltpu.VMEM((8, tokens), F32),
                pltpu.VMEM((WINDOW * tokens, tokens), BF16),
                pltpu.VMEM((WINDOW * tokens, tokens), BF16),
                pltpu.SemaphoreType.DMA((2 * PLANE + 2,)),
            ],
            compiler_params=params(),
            cost_estimate=cost(1 * heads),
        )(
            limits,
            *[part.reshape((2,) + shape) for part in key_held[chunk] + query_held[chunk]],
            even.reshape((2, 2) + shape),
            odd.reshape((2, 2) + shape),
        )

    def join(chunk, local, even, odd):
        heads = CHUNKS[chunk]
        flat = (2, heads * head_size, tokens)
        return pl.pallas_call(
            lambda *refs: join_kernel(size // PLANE, *refs),
            out_shape=[piece(heads)] * PLANE,
            in_specs=[VMEM] * 3,
            out_specs=[HBM] * PLANE,
            scratch_shapes=[
                pltpu.VMEM((PLANE,) + flat, BF16),
                pltpu.SemaphoreType.DMA((PLANE,)),
            ],
            compiler_params=params(),
        )(local.reshape((PLANE,) + flat), even.reshape((2,) + flat), odd.reshape((2,) + flat))

    results = [main(chunk) for chunk in range(rounds)]
    last = None
    returned = []
    for chunk in range(rounds):
        shape = (2, CHUNKS[chunk] * head_size, tokens)
        out = [part.reshape(shape) for part in results[chunk][:PLANE]]
        if chunk:
            out = after(out, last[1:] + list(returned[-1]))
        last = spread(out)
        query_pieces += last
        local, even, odd = results[chunk][PLANE:]
        returned.append((level_swap(even, 0), level_swap(odd, 1)))
    for chunk in range(rounds):
        local = results[chunk][PLANE]
        if chunk == rounds - 1:
            local = after([local], last[2:3] + [back[0]])[0]
        back = join(chunk, local, *returned[chunk])
        back = after(back, [] if chunk else [])
        key_pieces += spread(back)

    def finish(parts, chunks, held=()):
        span = PLANE * sum(CHUNKS[chunk] for chunk in chunks) * head_size
        return pl.pallas_call(
            lambda *refs: finish_kernel(head_size, chunks, len(held), *refs),
            out_shape=[jax.ShapeDtypeStruct((tokens, width), BF16)] * 2,
            in_specs=[HBM] * (len(parts) + len(held)),
            out_specs=[HBM, HBM],
            scratch_shapes=[
                pltpu.VMEM((2, span, tokens), BF16),
                pltpu.VMEM((2, tokens, span), BF16),
                pltpu.SemaphoreType.DMA((2, len(parts))),
                pltpu.SemaphoreType.DMA((2,)),
            ],
            input_output_aliases={len(parts) + index: index for index in range(len(held))},
            compiler_params=params(),
            cost_estimate=cost(3),
        )(*parts, *held)

    attended, query_grad = finish(query_pieces, every)
    sums = ()
    for chunk in every:
        sums = finish(key_pieces[PLANE * chunk : PLANE * (chunk + 1)], (chunk,), sums)
    return attended, query_grad, *sums


def solution(mesh):
    rows = P(("groups", "seq"), None)
    return jax.shard_map(
        body,
        mesh=mesh,
        in_specs=(rows, rows, rows, rows, P("groups", None), P("groups", None), P("groups")),
        out_specs=(rows, rows, rows, rows),
        check_vma=False,
    )
```

```python
import math

import jax
import jax.numpy as jnp
from jax import lax
from jax.experimental import pallas as pl
from jax.experimental.pallas import tpu as pltpu
from jax.sharding import PartitionSpec as P

HEADS = 16
BLK = 128
PLANE = 4
CHUNKS = (2, 2)
FAR_UP = 2
WINDOW = 4
CHAIN = PLANE + FAR_UP + 1
STRIP = 32
F32 = jnp.float32
BF16 = jnp.bfloat16
HBM = pl.BlockSpec(memory_space=pltpu.HBM)
SMEM = pl.BlockSpec(memory_space=pltpu.SMEM)
VMEM = pl.BlockSpec(memory_space=pltpu.VMEM)


def params(mib=64):
    return pltpu.CompilerParams(vmem_limit_bytes=mib << 20)


def after(arrays, others):
    if not others:
        return list(arrays)
    return list(lax.optimization_barrier((list(arrays), list(others)))[0])


def cost(microseconds):
    return pl.CostEstimate(
        flops=int(microseconds * 1_000_000_000), bytes_accessed=1_000_000, transcendentals=0
    )


def place_of():
    return lax.axis_index("seq") % PLANE


def level_of():
    return lax.axis_index("seq") // PLANE


def run_copies(copies):
    for copy in copies:
        copy.start()
    for copy in copies:
        copy.wait()


def prep_kernel(head_size, chunks, lists, first_in, second_in, *refs):
    lists_in, refs = refs[:lists], refs[lists:]
    count = PLANE * len(chunks)
    outs = refs[:count]
    rows, turned, in_sems, sems = refs[-4:]
    width = rows.shape[2]
    begin = PLANE * sum(CHUNKS[: chunks[0]]) * head_size
    loads = [
        pltpu.make_async_copy(ref.at[:, pl.ds(begin, width)], rows.at[index], in_sems.at[index])
        for index, ref in enumerate((first_in, second_in))
    ]
    for load in loads:
        load.start()
    if lists:
        find_limits(*lists_in, refs[count])
    place = place_of()
    copies = []
    for index, load in enumerate(loads):
        load.wait()
        turned[index] = rows[index].T
        first = 0
        for number, chunk in enumerate(chunks):
            span = CHUNKS[chunk] * head_size
            for hop in range(PLANE):
                row = pl.multiple_of(first + (place ^ hop) * span, 16)
                slot = number * PLANE + hop
                copy = pltpu.make_async_copy(
                    turned.at[index, pl.ds(row, span)],
                    outs[slot].at[index],
                    sems.at[index, slot],
                )
                copy.start()
                copies.append(copy)
            first += PLANE * span
    for copy in copies:
        copy.wait()


def find_limits(local_blocks, far_blocks, counts, out):
    blocks = counts.shape[0]
    first = level_of() * (PLANE * 2)
    for query in range(PLANE * 2):
        listed = [local_blocks[first + query, s] for s in range(local_blocks.shape[1])]
        listed += [far_blocks[first + query, s] for s in range(far_blocks.shape[1])]
        for slot in range(WINDOW * 2):
            key = first - 2 * FAR_UP + (query // 2) * 2 + slot
            found = listed[0] == key
            for entry in listed[1:]:
                found = found | (entry == key)
            inside = (key >= 0) & (key < blocks)
            count = counts[jnp.clip(key, 0, blocks - 1)]
            out[query * WINDOW * 2 + slot] = jnp.where(found & inside, count, 0)


def pack_kernel(*refs):
    pieces = refs[:PLANE]
    even, odd = refs[PLANE : PLANE + 2]
    plane, sems = refs[PLANE + 2 :]
    place, parity = place_of(), level_of() % 2
    run_copies(
        [
            pltpu.make_async_copy(pieces[hop], plane.at[place ^ hop], sems.at[hop])
            for hop in range(PLANE)
        ]
    )
    run_copies(
        [
            pltpu.make_async_copy(plane.at[pl.ds(2 - 2 * parity, 2)], even, sems.at[0]),
            pltpu.make_async_copy(plane.at[pl.ds(2 * parity, 2)], odd, sems.at[1]),
        ]
    )


def dot(a, b, left, right):
    return lax.dot_general(a, b, (((left,), (right,)), ((), ())), preferred_element_type=F32)


def main_kernel(head_size, heads, limits, *refs):
    key_pieces = refs[:PLANE]
    query_pieces = refs[PLANE : 2 * PLANE]
    even_in, odd_in = refs[2 * PLANE : 2 * PLANE + 2]
    rest = refs[2 * PLANE + 2 :]
    outs = rest[:PLANE]
    local_out, even_out, odd_out = rest[PLANE : PLANE + 3]
    chain, query, result, key_sums, sums = rest[PLANE + 3 : PLANE + 8]
    scores, grads, peaks = (rest[PLANE + 8 + 2 * i : PLANE + 10 + 2 * i] for i in range(3))
    weights, grad_scores, sems = rest[PLANE + 14 :]
    place, parity = place_of(), level_of() % 2
    copies = []
    for hop in range(PLANE):
        unit = place ^ hop
        copies.append(
            pltpu.make_async_copy(key_pieces[hop], chain.at[FAR_UP + unit], sems.at[2 * hop])
        )
        copies.append(
            pltpu.make_async_copy(query_pieces[hop], query.at[unit], sems.at[2 * hop + 1])
        )
    above = FAR_UP + PLANE
    copies.append(
        pltpu.make_async_copy(
            even_in, chain.at[pl.ds((1 - parity) * above, 2)], sems.at[2 * PLANE]
        )
    )
    copies.append(
        pltpu.make_async_copy(odd_in, chain.at[pl.ds(parity * above, 2)], sems.at[2 * PLANE + 1])
    )
    for copy in copies:
        copy.start()
    key_sums[...] = jnp.zeros_like(key_sums)
    for copy in copies:
        copy.wait()

    scale = 1.0 / math.sqrt(head_size)
    rate = scale * math.log2(math.e)
    tokens = 2 * BLK
    row = lax.broadcasted_iota(jnp.int32, (BLK, tokens), 0)
    lane = lax.broadcasted_iota(jnp.int32, (1, tokens), 1)
    steps = heads * PLANE

    def score(index, slot, k, peak):
        head, unit = index // PLANE, index % PLANE
        tile = dot(chain[unit + k, 0, head], query[unit, 0, head], 0, 0)
        for half in range(2):
            block = 2 * k + half
            base = unit * 2 * WINDOW * 2 + block
            limit = jnp.where(lane < BLK, limits[base], limits[base + WINDOW * 2])
            for at in range(0, BLK, STRIP):
                part = tile[half * BLK + at : half * BLK + at + STRIP]
                part = jnp.where(row[at : at + STRIP] < limit, part, -1e30)
                top = jnp.max(part.reshape(STRIP // 8, 8, tokens), axis=0)
                peak = top if peak is None else jnp.maximum(peak, top)
                scores[slot][block * BLK + at : block * BLK + at + STRIP] = part
        return peak

    def keep_peak(slot, peak):
        peak = jnp.max(peak, axis=0, keepdims=True)
        peaks[slot][...] = jnp.broadcast_to(peak, (8, tokens))

    def grad(index, slot, k):
        head, unit = index // PLANE, index % PLANE
        grads[slot][k * tokens : (k + 1) * tokens] = dot(
            chain[unit + k, 1, head], query[unit, 1, head], 0, 0
        )

    def step(index, now, later, final=False):
        head, unit = index // PLANE, index % PLANE
        query_t = query[unit, 0, head]
        grad_wide = query[unit, 1, head].astype(F32)
        peak = peaks[now][0:1]
        total = out_t = later_peak = query_grad = None
        for k in range(WINDOW):
            span = slice(k * tokens, (k + 1) * tokens)
            if not final:
                later_peak = score(index + 1, later, k, later_peak)
            for at in range(k * tokens, (k + 1) * tokens, STRIP):
                power = jnp.exp2((scores[now][at : at + STRIP] - peak) * rate)
                part = jnp.sum(power.reshape(STRIP // 8, 8, tokens), axis=0)
                total = part if total is None else total + part
                weights[at : at + STRIP] = power.astype(BF16)
            part = dot(chain[unit + k, 1, head], weights[span], 1, 0)
            out_t = part if k == 0 else out_t + part
        if not final:
            keep_peak(later, later_peak)
        inverse = 1.0 / jnp.sum(total, axis=0, keepdims=True)
        attended = (out_t * inverse).astype(BF16)
        delta = jnp.sum(grad_wide * attended.astype(F32), axis=0, keepdims=True)
        grad_scaled = (grad_wide * inverse).astype(BF16)
        query_scaled = (query_t.astype(F32) * inverse).astype(BF16)
        for k in range(WINDOW):
            span = slice(k * tokens, (k + 1) * tokens)
            key_sums[unit + k, 1, head] += dot(grad_scaled, weights[span], 1, 1)
        for k in range(WINDOW):
            span = slice(k * tokens, (k + 1) * tokens)
            if not final:
                grad(index + 1, later, k)
            for at in range(k * tokens, (k + 1) * tokens, STRIP):
                change = (grads[now][at : at + STRIP] - delta).astype(BF16)
                grad_scores[at : at + STRIP] = weights[at : at + STRIP] * change
            part = dot(chain[unit + k, 0, head], grad_scores[span], 1, 0)
            query_grad = part if k == 0 else query_grad + part
            key_sums[unit + k, 0, head] += dot(query_scaled, grad_scores[span], 1, 1)
        result[unit, 0, head] = attended
        result[unit, 1, head] = (query_grad * (inverse * scale)).astype(BF16)

    first_peak = None
    for k in range(WINDOW):
        first_peak = score(0, 0, k, first_peak)
        grad(0, 0, k)
    keep_peak(0, first_peak)

    def two_steps(index, carry):
        step(2 * index, 0, 1)
        step(2 * index + 1, 1, 0)
        return carry

    lax.fori_loop(0, steps // 2 - 1, two_steps, 0)
    step(steps - 2, 0, 1)
    step(steps - 1, 1, 0, final=True)
    copies = [
        pltpu.make_async_copy(result.at[place ^ hop], outs[hop], sems.at[hop])
        for hop in range(PLANE)
    ]
    for copy in copies:
        copy.start()
    for unit in range(CHAIN + 1):
        sums[unit, 0] = (key_sums[unit, 0] * scale).astype(BF16)
        sums[unit, 1] = key_sums[unit, 1].astype(BF16)
    more = [
        pltpu.make_async_copy(sums.at[pl.ds(FAR_UP, PLANE)], local_out, sems.at[PLANE]),
        pltpu.make_async_copy(
            sums.at[pl.ds((1 - parity) * above, 2)], even_out, sems.at[PLANE + 1]
        ),
        pltpu.make_async_copy(sums.at[pl.ds(parity * above, 2)], odd_out, sems.at[PLANE + 2]),
    ]
    for copy in more:
        copy.start()
    for copy in copies + more:
        copy.wait()


def join_kernel(planes, local, even_in, odd_in, *refs):
    outs = refs[:PLANE]
    held, even, odd, sems = refs[PLANE:]
    place, parity = place_of(), level_of() % 2
    level = level_of()
    run_copies(
        [
            pltpu.make_async_copy(local, held, sems.at[0]),
            pltpu.make_async_copy(even_in, even, sems.at[1]),
            pltpu.make_async_copy(odd_in, odd, sems.at[2]),
        ]
    )

    def add(unit, part):
        held[unit] = (held[unit].astype(F32) + part.astype(F32)).astype(BF16)

    def take(below, above):
        @pl.when(level > 0)
        def _():
            add(0, below[0])

        @pl.when(level < planes - 1)
        def _():
            add(2, above[0])
            add(3, above[1])

    @pl.when(parity == 0)
    def _():
        take(odd, even)

    @pl.when(parity == 1)
    def _():
        take(even, odd)

    run_copies(
        [
            pltpu.make_async_copy(held.at[place ^ hop], outs[hop], sems.at[hop])
            for hop in range(PLANE)
        ]
    )


def finish_kernel(head_size, chunks, held, *refs):
    count = PLANE * len(chunks)
    pieces = refs[:count]
    outs = refs[count + held : count + held + 2]
    turned, rows, sems, out_sems = refs[count + held + 2 :]
    place = place_of()
    begin = PLANE * sum(CHUNKS[: chunks[0]]) * head_size
    width = rows.shape[2]
    loads = []
    first = 0
    for number, chunk in enumerate(chunks):
        span = CHUNKS[chunk] * head_size
        for hop in range(PLANE):
            row = pl.multiple_of(first + (place ^ hop) * span, 16)
            for tensor in range(2):
                loads.append(
                    pltpu.make_async_copy(
                        pieces[number * PLANE + hop].at[tensor],
                        turned.at[tensor, pl.ds(row, span)],
                        sems.at[tensor, number * PLANE + hop],
                    )
                )
        first += PLANE * span
    for load in loads:
        load.start()
    stores = []
    for tensor in range(2):
        for load in loads[tensor::2]:
            load.wait()
        rows[tensor] = turned[tensor].T
        store = pltpu.make_async_copy(
            rows.at[tensor], outs[tensor].at[:, pl.ds(begin, width)], out_sems.at[tensor]
        )
        store.start()
        stores.append(store)
    for store in stores:
        store.wait()


def body(queries, keys, values, cotangent, local_blocks, far_blocks, counts):
    tokens, width = queries.shape
    head_size = width // HEADS
    size = lax.axis_size("seq")
    planes = size // PLANE
    def swap(array, hop):
        pairs = [(i, (i // PLANE) * PLANE + ((i % PLANE) ^ hop)) for i in range(size)]
        return lax.ppermute(array, "seq", pairs)

    def level_swap(array, odd):
        pairs = []
        for i in range(size):
            z = i // PLANE
            other = z + 1 if z % 2 == odd else z - 1
            pairs.append((i, i + (other - z) * PLANE if 0 <= other < planes else i ^ 1))
        return lax.ppermute(array, "seq", pairs)

    def piece(heads):
        return jax.ShapeDtypeStruct((2, heads * head_size, tokens), BF16)

    def prep(first, second, chunks, *lists):
        span = PLANE * sum(CHUNKS[chunk] for chunk in chunks) * head_size
        limits_shape = jax.ShapeDtypeStruct((PLANE * 2 * WINDOW * 2,), jnp.int32)
        count = PLANE * len(chunks)
        return pl.pallas_call(
            lambda *refs: prep_kernel(head_size, chunks, len(lists), *refs),
            out_shape=[piece(CHUNKS[chunk]) for chunk in chunks for _ in range(PLANE)]
            + ([limits_shape] if lists else []),
            in_specs=[HBM, HBM] + [SMEM] * len(lists),
            out_specs=[HBM] * count + ([SMEM] if lists else []),
            scratch_shapes=[
                pltpu.VMEM((2, tokens, span), BF16),
                pltpu.VMEM((2, span, tokens), BF16),
                pltpu.SemaphoreType.DMA((2,)),
                pltpu.SemaphoreType.DMA((2, count)),
            ],
            compiler_params=params(),
            cost_estimate=cost(12),
        )(first, second, *lists)

    def spread(parts):
        moved = {hop: swap(parts[hop], hop) for hop in (1, 2, 3)}
        return [parts[0]] + [moved[hop] for hop in range(1, PLANE)]

    rounds = len(CHUNKS)
    every = tuple(range(rounds))
    key_held = [
        spread(key_ready[PLANE * chunk : PLANE * (chunk + 1)])
        for key_ready in [prep(keys, values, every)]
        for chunk in every
    ]
    query_pieces = []
    key_pieces = []
    halos = []
    *query_ready, limits = prep(queries, cotangent, every, local_blocks, far_blocks, counts)
    query_held = [spread(query_ready[PLANE * chunk : PLANE * (chunk + 1)]) for chunk in every]
    for chunk, heads in enumerate(CHUNKS):
        held = key_held[chunk]
        held = after(held, query_ready if chunk else query_ready)
        pair = jax.ShapeDtypeStruct((2, 2, heads * head_size, tokens), BF16)
        even, odd = pl.pallas_call(
            pack_kernel,
            out_shape=[pair, pair],
            in_specs=[HBM] * PLANE,
            out_specs=[HBM, HBM],
            scratch_shapes=[
                pltpu.VMEM((PLANE, 2, heads * head_size, tokens), BF16),
                pltpu.SemaphoreType.DMA((PLANE,)),
            ],
            compiler_params=params(),
            cost_estimate=cost(2),
        )(*held)
        halos.append((level_swap(even, 0), level_swap(odd, 1)))

    def main(chunk):
        heads = CHUNKS[chunk]
        even, odd = halos[chunk]
        shape = (heads, head_size, tokens)
        return pl.pallas_call(
            lambda *refs: main_kernel(head_size, heads, *refs),
            out_shape=[jax.ShapeDtypeStruct((2,) + shape, BF16)] * PLANE
            + [jax.ShapeDtypeStruct((PLANE, 2) + shape, BF16)]
            + [jax.ShapeDtypeStruct((2, 2) + shape, BF16)] * 2,
            in_specs=[SMEM] + [HBM] * (2 * PLANE + 2),
            out_specs=[HBM] * (PLANE + 3),
            scratch_shapes=[
                pltpu.VMEM((CHAIN + 1, 2) + shape, BF16),
                pltpu.VMEM((PLANE, 2) + shape, BF16),
                pltpu.VMEM((PLANE, 2) + shape, BF16),
                pltpu.VMEM((CHAIN + 1, 2) + shape, F32),
                pltpu.VMEM((CHAIN + 1, 2) + shape, BF16),
                pltpu.VMEM((WINDOW * tokens, tokens), F32),
                pltpu.VMEM((WINDOW * tokens, tokens), F32),
                pltpu.VMEM((WINDOW * tokens, tokens), F32),
                pltpu.VMEM((WINDOW * tokens, tokens), F32),
                pltpu.VMEM((8, tokens), F32),
                pltpu.VMEM((8, tokens), F32),
                pltpu.VMEM((WINDOW * tokens, tokens), BF16),
                pltpu.VMEM((WINDOW * tokens, tokens), BF16),
                pltpu.SemaphoreType.DMA((2 * PLANE + 2,)),
            ],
            compiler_params=params(),
            cost_estimate=cost(1 * heads),
        )(
            limits,
            *[part.reshape((2,) + shape) for part in key_held[chunk] + query_held[chunk]],
            even.reshape((2, 2) + shape),
            odd.reshape((2, 2) + shape),
        )

    def join(chunk, local, even, odd):
        heads = CHUNKS[chunk]
        flat = (2, heads * head_size, tokens)
        return pl.pallas_call(
            lambda *refs: join_kernel(size // PLANE, *refs),
            out_shape=[piece(heads)] * PLANE,
            in_specs=[HBM] * 3,
            out_specs=[HBM] * PLANE,
            scratch_shapes=[
                pltpu.VMEM((PLANE,) + flat, BF16),
                pltpu.VMEM((2,) + flat, BF16),
                pltpu.VMEM((2,) + flat, BF16),
                pltpu.SemaphoreType.DMA((PLANE,)),
            ],
            compiler_params=params(),
        )(local.reshape((PLANE,) + flat), even.reshape((2,) + flat), odd.reshape((2,) + flat))

    results = [main(chunk) for chunk in range(rounds)]
    last = None
    returned = []
    for chunk in range(rounds):
        shape = (2, CHUNKS[chunk] * head_size, tokens)
        out = [part.reshape(shape) for part in results[chunk][:PLANE]]
        if chunk:
            out = after(out, last[1:] + list(returned[-1]))
        last = spread(out)
        query_pieces += last
        local, even, odd = results[chunk][PLANE:]
        returned.append((level_swap(even, 0), level_swap(odd, 1)))
    for chunk in range(rounds):
        local = results[chunk][PLANE]
        if chunk == rounds - 1:
            local = after([local], last[2:3] + [back[0]])[0]
        back = join(chunk, local, *returned[chunk])
        back = after(back, [] if chunk else [])
        key_pieces += spread(back)

    def finish(parts, chunks, held=()):
        span = PLANE * sum(CHUNKS[chunk] for chunk in chunks) * head_size
        return pl.pallas_call(
            lambda *refs: finish_kernel(head_size, chunks, len(held), *refs),
            out_shape=[jax.ShapeDtypeStruct((tokens, width), BF16)] * 2,
            in_specs=[HBM] * (len(parts) + len(held)),
            out_specs=[HBM, HBM],
            scratch_shapes=[
                pltpu.VMEM((2, span, tokens), BF16),
                pltpu.VMEM((2, tokens, span), BF16),
                pltpu.SemaphoreType.DMA((2, len(parts))),
                pltpu.SemaphoreType.DMA((2,)),
            ],
            input_output_aliases={len(parts) + index: index for index in range(len(held))},
            compiler_params=params(),
            cost_estimate=cost(8),
        )(*parts, *held)

    attended, query_grad = finish(query_pieces, every)
    sums = ()
    for chunk in every:
        sums = finish(key_pieces[PLANE * chunk : PLANE * (chunk + 1)], (chunk,), sums)
    return attended, query_grad, *sums


def solution(mesh):
    rows = P(("groups", "seq"), None)
    return jax.shard_map(
        body,
        mesh=mesh,
        in_specs=(rows, rows, rows, rows, P("groups", None), P("groups", None), P("groups")),
        out_specs=(rows, rows, rows, rows),
        check_vma=False,
    )
```

```python
import math

import jax
import jax.numpy as jnp
from jax import lax
from jax.experimental import pallas as pl
from jax.experimental.pallas import tpu as pltpu
from jax.sharding import PartitionSpec as P

HEADS = 16
BLK = 128
PLANE = 4
CHUNKS = (2, 2)
FAR_UP = 2
WINDOW = 4
CHAIN = PLANE + FAR_UP + 1
STRIP = 32
F32 = jnp.float32
BF16 = jnp.bfloat16
HBM = pl.BlockSpec(memory_space=pltpu.HBM)
SMEM = pl.BlockSpec(memory_space=pltpu.SMEM)
VMEM = pl.BlockSpec(memory_space=pltpu.VMEM)


def params(mib=64):
    return pltpu.CompilerParams(vmem_limit_bytes=mib << 20)


def after(arrays, others):
    if not others:
        return list(arrays)
    return list(lax.optimization_barrier((list(arrays), list(others)))[0])


def cost(microseconds):
    return pl.CostEstimate(
        flops=int(microseconds * 1_000_000_000), bytes_accessed=1_000_000, transcendentals=0
    )


def place_of():
    return lax.axis_index("seq") % PLANE


def level_of():
    return lax.axis_index("seq") // PLANE


def run_copies(copies):
    for copy in copies:
        copy.start()
    for copy in copies:
        copy.wait()


def prep_kernel(head_size, chunks, lists, first_in, second_in, *refs):
    lists_in, refs = refs[:lists], refs[lists:]
    count = PLANE * len(chunks)
    outs = refs[:count]
    rows, turned, in_sems, sems = refs[-4:]
    width = rows.shape[2]
    begin = PLANE * sum(CHUNKS[: chunks[0]]) * head_size
    loads = [
        pltpu.make_async_copy(ref.at[:, pl.ds(begin, width)], rows.at[index], in_sems.at[index])
        for index, ref in enumerate((first_in, second_in))
    ]
    for load in loads:
        load.start()
    if lists:
        find_limits(*lists_in, refs[count])
    for index, load in enumerate(loads):
        load.wait()
        turned[index] = rows[index].T
    place = place_of()
    copies = []
    first = 0
    for number, chunk in enumerate(chunks):
        span = CHUNKS[chunk] * head_size
        for hop in range(PLANE):
            row = pl.multiple_of(first + (place ^ hop) * span, 16)
            slot = number * PLANE + hop
            copies.append(
                pltpu.make_async_copy(
                    turned.at[:, pl.ds(row, span)], outs[slot], sems.at[slot]
                )
            )
        first += PLANE * span
    run_copies(copies)


def find_limits(local_blocks, far_blocks, counts, out):
    blocks = counts.shape[0]
    first = level_of() * (PLANE * 2)
    for query in range(PLANE * 2):
        listed = [local_blocks[first + query, s] for s in range(local_blocks.shape[1])]
        listed += [far_blocks[first + query, s] for s in range(far_blocks.shape[1])]
        for slot in range(WINDOW * 2):
            key = first - 2 * FAR_UP + (query // 2) * 2 + slot
            found = listed[0] == key
            for entry in listed[1:]:
                found = found | (entry == key)
            inside = (key >= 0) & (key < blocks)
            count = counts[jnp.clip(key, 0, blocks - 1)]
            out[query * WINDOW * 2 + slot] = jnp.where(found & inside, count, 0)


def pack_kernel(*refs):
    pieces = refs[:PLANE]
    even, odd = refs[PLANE : PLANE + 2]
    plane, sems = refs[PLANE + 2 :]
    place, parity = place_of(), level_of() % 2
    run_copies(
        [
            pltpu.make_async_copy(pieces[hop], plane.at[place ^ hop], sems.at[hop])
            for hop in range(PLANE)
        ]
    )
    run_copies(
        [
            pltpu.make_async_copy(plane.at[pl.ds(2 - 2 * parity, 2)], even, sems.at[0]),
            pltpu.make_async_copy(plane.at[pl.ds(2 * parity, 2)], odd, sems.at[1]),
        ]
    )


def dot(a, b, left, right):
    return lax.dot_general(a, b, (((left,), (right,)), ((), ())), preferred_element_type=F32)


def main_kernel(head_size, heads, limits, *refs):
    key_pieces = refs[:PLANE]
    query_pieces = refs[PLANE : 2 * PLANE]
    even_in, odd_in = refs[2 * PLANE : 2 * PLANE + 2]
    rest = refs[2 * PLANE + 2 :]
    outs = rest[:PLANE]
    local_out, even_out, odd_out = rest[PLANE : PLANE + 3]
    chain, query, result, key_sums, sums = rest[PLANE + 3 : PLANE + 8]
    scores, grads, peaks = (rest[PLANE + 8 + 2 * i : PLANE + 10 + 2 * i] for i in range(3))
    weights, grad_scores, sems = rest[PLANE + 14 :]
    place, parity = place_of(), level_of() % 2
    copies = []
    for hop in range(PLANE):
        unit = place ^ hop
        copies.append(
            pltpu.make_async_copy(key_pieces[hop], chain.at[FAR_UP + unit], sems.at[2 * hop])
        )
        copies.append(
            pltpu.make_async_copy(query_pieces[hop], query.at[unit], sems.at[2 * hop + 1])
        )
    above = FAR_UP + PLANE
    copies.append(
        pltpu.make_async_copy(
            even_in, chain.at[pl.ds((1 - parity) * above, 2)], sems.at[2 * PLANE]
        )
    )
    copies.append(
        pltpu.make_async_copy(odd_in, chain.at[pl.ds(parity * above, 2)], sems.at[2 * PLANE + 1])
    )
    for copy in copies:
        copy.start()
    key_sums[...] = jnp.zeros_like(key_sums)
    for copy in copies:
        copy.wait()

    scale = 1.0 / math.sqrt(head_size)
    rate = scale * math.log2(math.e)
    tokens = 2 * BLK
    row = lax.broadcasted_iota(jnp.int32, (BLK, tokens), 0)
    lane = lax.broadcasted_iota(jnp.int32, (1, tokens), 1)
    steps = heads * PLANE

    def score(index, slot, k, peak):
        head, unit = index // PLANE, index % PLANE
        tile = dot(chain[unit + k, 0, head], query[unit, 0, head], 0, 0)
        for half in range(2):
            block = 2 * k + half
            base = unit * 2 * WINDOW * 2 + block
            limit = jnp.where(lane < BLK, limits[base], limits[base + WINDOW * 2])
            for at in range(0, BLK, STRIP):
                part = tile[half * BLK + at : half * BLK + at + STRIP]
                part = jnp.where(row[at : at + STRIP] < limit, part, -1e30)
                top = jnp.max(part.reshape(STRIP // 8, 8, tokens), axis=0)
                peak = top if peak is None else jnp.maximum(peak, top)
                scores[slot][block * BLK + at : block * BLK + at + STRIP] = part
        return peak

    def keep_peak(slot, peak):
        peak = jnp.max(peak, axis=0, keepdims=True)
        peaks[slot][...] = jnp.broadcast_to(peak, (8, tokens))

    def grad(index, slot, k):
        head, unit = index // PLANE, index % PLANE
        grads[slot][k * tokens : (k + 1) * tokens] = dot(
            chain[unit + k, 1, head], query[unit, 1, head], 0, 0
        )

    def step(index, now, later, final=False):
        head, unit = index // PLANE, index % PLANE
        query_t = query[unit, 0, head]
        grad_wide = query[unit, 1, head].astype(F32)
        peak = peaks[now][0:1]
        total = out_t = later_peak = query_grad = None
        for k in range(WINDOW):
            span = slice(k * tokens, (k + 1) * tokens)
            if not final:
                later_peak = score(index + 1, later, k, later_peak)
            for at in range(k * tokens, (k + 1) * tokens, STRIP):
                power = jnp.exp2((scores[now][at : at + STRIP] - peak) * rate)
                part = jnp.sum(power.reshape(STRIP // 8, 8, tokens), axis=0)
                total = part if total is None else total + part
                weights[at : at + STRIP] = power.astype(BF16)
            part = dot(chain[unit + k, 1, head], weights[span], 1, 0)
            out_t = part if k == 0 else out_t + part
        if not final:
            keep_peak(later, later_peak)
        inverse = 1.0 / jnp.sum(total, axis=0, keepdims=True)
        attended = (out_t * inverse).astype(BF16)
        delta = jnp.sum(grad_wide * attended.astype(F32), axis=0, keepdims=True)
        grad_scaled = (grad_wide * inverse).astype(BF16)
        query_scaled = (query_t.astype(F32) * inverse).astype(BF16)
        for k in range(WINDOW):
            span = slice(k * tokens, (k + 1) * tokens)
            key_sums[unit + k, 1, head] += dot(grad_scaled, weights[span], 1, 1)
        for k in range(WINDOW):
            span = slice(k * tokens, (k + 1) * tokens)
            if not final:
                grad(index + 1, later, k)
            for at in range(k * tokens, (k + 1) * tokens, STRIP):
                change = (grads[now][at : at + STRIP] - delta).astype(BF16)
                grad_scores[at : at + STRIP] = weights[at : at + STRIP] * change
            part = dot(chain[unit + k, 0, head], grad_scores[span], 1, 0)
            query_grad = part if k == 0 else query_grad + part
            key_sums[unit + k, 0, head] += dot(query_scaled, grad_scores[span], 1, 1)
        result[unit, 0, head] = attended
        result[unit, 1, head] = (query_grad * (inverse * scale)).astype(BF16)

    first_peak = None
    for k in range(WINDOW):
        first_peak = score(0, 0, k, first_peak)
        grad(0, 0, k)
    keep_peak(0, first_peak)

    def two_steps(index, carry):
        step(2 * index, 0, 1)
        step(2 * index + 1, 1, 0)
        return carry

    lax.fori_loop(0, steps // 2 - 1, two_steps, 0)
    step(steps - 2, 0, 1)
    step(steps - 1, 1, 0, final=True)
    copies = [
        pltpu.make_async_copy(result.at[place ^ hop], outs[hop], sems.at[hop])
        for hop in range(PLANE)
    ]
    for copy in copies:
        copy.start()
    for unit in range(CHAIN + 1):
        sums[unit, 0] = (key_sums[unit, 0] * scale).astype(BF16)
        sums[unit, 1] = key_sums[unit, 1].astype(BF16)
    more = [
        pltpu.make_async_copy(sums.at[pl.ds(FAR_UP, PLANE)], local_out, sems.at[PLANE]),
        pltpu.make_async_copy(
            sums.at[pl.ds((1 - parity) * above, 2)], even_out, sems.at[PLANE + 1]
        ),
        pltpu.make_async_copy(sums.at[pl.ds(parity * above, 2)], odd_out, sems.at[PLANE + 2]),
    ]
    for copy in more:
        copy.start()
    for copy in copies + more:
        copy.wait()


def join_kernel(planes, local, even_in, odd_in, *refs):
    outs = refs[:PLANE]
    held, sems = refs[PLANE:]
    place, parity = place_of(), level_of() % 2
    level = level_of()
    held[...] = local[...]

    def take(below, above):
        @pl.when(level > 0)
        def _():
            held[0] = (held[0].astype(F32) + below[0].astype(F32)).astype(BF16)

        @pl.when(level < planes - 1)
        def _():
            for unit in range(2):
                held[2 + unit] = (held[2 + unit].astype(F32) + above[unit].astype(F32)).astype(
                    BF16
                )

    @pl.when(parity == 0)
    def _():
        take(odd_in, even_in)

    @pl.when(parity == 1)
    def _():
        take(even_in, odd_in)

    run_copies(
        [
            pltpu.make_async_copy(held.at[place ^ hop], outs[hop], sems.at[hop])
            for hop in range(PLANE)
        ]
    )


def finish_kernel(head_size, chunks, held, *refs):
    count = PLANE * len(chunks)
    pieces = refs[:count]
    outs = refs[count + held : count + held + 2]
    turned, rows, sems, out_sems = refs[count + held + 2 :]
    place = place_of()
    begin = PLANE * sum(CHUNKS[: chunks[0]]) * head_size
    width = rows.shape[2]
    loads = []
    first = 0
    for number, chunk in enumerate(chunks):
        span = CHUNKS[chunk] * head_size
        for hop in range(PLANE):
            row = pl.multiple_of(first + (place ^ hop) * span, 16)
            for tensor in range(2):
                loads.append(
                    pltpu.make_async_copy(
                        pieces[number * PLANE + hop].at[tensor],
                        turned.at[tensor, pl.ds(row, span)],
                        sems.at[tensor, number * PLANE + hop],
                    )
                )
        first += PLANE * span
    for load in loads:
        load.start()
    stores = []
    for tensor in range(2):
        for load in loads[tensor::2]:
            load.wait()
        rows[tensor] = turned[tensor].T
        store = pltpu.make_async_copy(
            rows.at[tensor], outs[tensor].at[:, pl.ds(begin, width)], out_sems.at[tensor]
        )
        store.start()
        stores.append(store)
    for store in stores:
        store.wait()


def body(queries, keys, values, cotangent, local_blocks, far_blocks, counts):
    tokens, width = queries.shape
    head_size = width // HEADS
    size = lax.axis_size("seq")
    planes = size // PLANE
    def swap(array, hop):
        pairs = [(i, (i // PLANE) * PLANE + ((i % PLANE) ^ hop)) for i in range(size)]
        return lax.ppermute(array, "seq", pairs)

    def level_swap(array, odd):
        pairs = []
        for i in range(size):
            z = i // PLANE
            other = z + 1 if z % 2 == odd else z - 1
            pairs.append((i, i + (other - z) * PLANE if 0 <= other < planes else i ^ 1))
        return lax.ppermute(array, "seq", pairs)

    def piece(heads):
        return jax.ShapeDtypeStruct((2, heads * head_size, tokens), BF16)

    def prep(first, second, chunks, *lists):
        span = PLANE * sum(CHUNKS[chunk] for chunk in chunks) * head_size
        limits_shape = jax.ShapeDtypeStruct((PLANE * 2 * WINDOW * 2,), jnp.int32)
        count = PLANE * len(chunks)
        return pl.pallas_call(
            lambda *refs: prep_kernel(head_size, chunks, len(lists), *refs),
            out_shape=[piece(CHUNKS[chunk]) for chunk in chunks for _ in range(PLANE)]
            + ([limits_shape] if lists else []),
            in_specs=[HBM, HBM] + [SMEM] * len(lists),
            out_specs=[HBM] * count + ([SMEM] if lists else []),
            scratch_shapes=[
                pltpu.VMEM((2, tokens, span), BF16),
                pltpu.VMEM((2, span, tokens), BF16),
                pltpu.SemaphoreType.DMA((2,)),
                pltpu.SemaphoreType.DMA((count,)),
            ],
            compiler_params=params(),
            cost_estimate=cost(3),
        )(first, second, *lists)

    def spread(parts):
        moved = {hop: swap(parts[hop], hop) for hop in (1, 2, 3)}
        return [parts[0]] + [moved[hop] for hop in range(1, PLANE)]

    rounds = len(CHUNKS)
    every = tuple(range(rounds))
    key_held = [
        spread(key_ready[PLANE * chunk : PLANE * (chunk + 1)])
        for key_ready in [prep(keys, values, every)]
        for chunk in every
    ]
    query_pieces = []
    key_pieces = []
    halos = []
    *query_ready, limits = prep(queries, cotangent, every, local_blocks, far_blocks, counts)
    query_held = [spread(query_ready[PLANE * chunk : PLANE * (chunk + 1)]) for chunk in every]
    for chunk, heads in enumerate(CHUNKS):
        held = key_held[chunk]
        held = after(held, query_ready if chunk else query_ready)
        pair = jax.ShapeDtypeStruct((2, 2, heads * head_size, tokens), BF16)
        even, odd = pl.pallas_call(
            pack_kernel,
            out_shape=[pair, pair],
            in_specs=[HBM] * PLANE,
            out_specs=[HBM, HBM],
            scratch_shapes=[
                pltpu.VMEM((PLANE, 2, heads * head_size, tokens), BF16),
                pltpu.SemaphoreType.DMA((PLANE,)),
            ],
            compiler_params=params(),
            cost_estimate=cost(2),
        )(*held)
        halos.append((level_swap(even, 0), level_swap(odd, 1)))

    def main(chunk):
        heads = CHUNKS[chunk]
        even, odd = halos[chunk]
        shape = (heads, head_size, tokens)
        return pl.pallas_call(
            lambda *refs: main_kernel(head_size, heads, *refs),
            out_shape=[jax.ShapeDtypeStruct((2,) + shape, BF16)] * PLANE
            + [jax.ShapeDtypeStruct((PLANE, 2) + shape, BF16)]
            + [jax.ShapeDtypeStruct((2, 2) + shape, BF16)] * 2,
            in_specs=[SMEM] + [HBM] * (2 * PLANE + 2),
            out_specs=[HBM] * (PLANE + 3),
            scratch_shapes=[
                pltpu.VMEM((CHAIN + 1, 2) + shape, BF16),
                pltpu.VMEM((PLANE, 2) + shape, BF16),
                pltpu.VMEM((PLANE, 2) + shape, BF16),
                pltpu.VMEM((CHAIN + 1, 2) + shape, F32),
                pltpu.VMEM((CHAIN + 1, 2) + shape, BF16),
                pltpu.VMEM((WINDOW * tokens, tokens), F32),
                pltpu.VMEM((WINDOW * tokens, tokens), F32),
                pltpu.VMEM((WINDOW * tokens, tokens), F32),
                pltpu.VMEM((WINDOW * tokens, tokens), F32),
                pltpu.VMEM((8, tokens), F32),
                pltpu.VMEM((8, tokens), F32),
                pltpu.VMEM((WINDOW * tokens, tokens), BF16),
                pltpu.VMEM((WINDOW * tokens, tokens), BF16),
                pltpu.SemaphoreType.DMA((2 * PLANE + 2,)),
            ],
            compiler_params=params(),
            cost_estimate=cost(1 * heads),
        )(
            limits,
            *[part.reshape((2,) + shape) for part in key_held[chunk] + query_held[chunk]],
            even.reshape((2, 2) + shape),
            odd.reshape((2, 2) + shape),
        )

    def join(chunk, local, even, odd):
        heads = CHUNKS[chunk]
        flat = (2, heads * head_size, tokens)
        return pl.pallas_call(
            lambda *refs: join_kernel(size // PLANE, *refs),
            out_shape=[piece(heads)] * PLANE,
            in_specs=[VMEM] * 3,
            out_specs=[HBM] * PLANE,
            scratch_shapes=[
                pltpu.VMEM((PLANE,) + flat, BF16),
                pltpu.SemaphoreType.DMA((PLANE,)),
            ],
            compiler_params=params(),
        )(local.reshape((PLANE,) + flat), even.reshape((2,) + flat), odd.reshape((2,) + flat))

    results = [main(chunk) for chunk in range(rounds)]
    last = None
    returned = []
    for chunk in range(rounds):
        shape = (2, CHUNKS[chunk] * head_size, tokens)
        out = [part.reshape(shape) for part in results[chunk][:PLANE]]
        if chunk:
            out = after(out, last[1:] + list(returned[-1]))
        last = spread(out)
        query_pieces += last
        local, even, odd = results[chunk][PLANE:]
        returned.append((level_swap(even, 0), level_swap(odd, 1)))
    for chunk in range(rounds):
        local = results[chunk][PLANE]
        if chunk == rounds - 1:
            local = after([local], last[2:3] + [back[0]])[0]
        back = join(chunk, local, *returned[chunk])
        back = after(back, [] if chunk else [])
        key_pieces += spread(back)

    def finish(parts, chunks, held=()):
        span = PLANE * sum(CHUNKS[chunk] for chunk in chunks) * head_size
        return pl.pallas_call(
            lambda *refs: finish_kernel(head_size, chunks, len(held), *refs),
            out_shape=[jax.ShapeDtypeStruct((tokens, width), BF16)] * 2,
            in_specs=[HBM] * (len(parts) + len(held)),
            out_specs=[HBM, HBM],
            scratch_shapes=[
                pltpu.VMEM((2, span, tokens), BF16),
                pltpu.VMEM((2, tokens, span), BF16),
                pltpu.SemaphoreType.DMA((2, len(parts))),
                pltpu.SemaphoreType.DMA((2,)),
            ],
            input_output_aliases={len(parts) + index: index for index in range(len(held))},
            compiler_params=params(),
            cost_estimate=cost(3),
        )(*parts, *held)

    attended, query_grad = finish(query_pieces, every)
    sums = ()
    for chunk in every:
        sums = finish(key_pieces[PLANE * chunk : PLANE * (chunk + 1)], (chunk,), sums)
    return attended, query_grad, *sums


def solution(mesh):
    rows = P(("groups", "seq"), None)
    return jax.shard_map(
        body,
        mesh=mesh,
        in_specs=(rows, rows, rows, rows, P("groups", None), P("groups", None), P("groups")),
        out_specs=(rows, rows, rows, rows),
        check_vma=False,
    )
```
